128 devices in a mesh: dp: 4 (over z), ctx: 32 (over y, x, core).
Axes of the slice: x: 4, y: 4, z: 4, core: 2. Of those that a mesh axis runs over, the one named last changes fastest.
Arguments:
- generated_input: bfloat16 [4, 4096, 8192], P('dp', 'ctx'), may hold values from -6 to 6
- frozen_query: bfloat16 [4, 4096, 4096], P('dp', 'ctx'), may hold values from -12 to 12
- frozen_key_value: bfloat16 [4, 4096, 1024], P('dp', 'ctx'), may hold values from -6 to 6
- adapter_down_weight: bfloat16 [8192, 128], replicated, may hold values from -0.0625 to 0.0625
- query_up_weight: bfloat16 [64, 4096], replicated, may hold values from -0.75 to 0.75
- value_up_weight: bfloat16 [64, 512], replicated, may hold values from -0.75 to 0.75
- response_numbers: int32 [4, 4096], P('dp', 'ctx'), may hold values from 0 to 3, never falling along the last dimension, each value on 1 to 3072 neighbouring positions
- target_replica: int32 [32, 4, 4], P('ctx'), may hold values from 0 to 3, as said below
- output_gradient: bfloat16 [4, 4096, 4096], P('dp', 'ctx'), may hold values from -6 to 6
Outputs:
- attn_out: bfloat16 [4, 4096, 4096], P('dp', 'ctx')
- grad_a: float32 [8192, 128], replicated
- query_up_gradient: float32 [64, 4096], replicated
- value_up_gradient: float32 [64, 512], replicated
The draws below stay inside these ranges and needn't reach their ends.
Inputs may be any that keep to these rules, and one draw needn't show every extreme that they name: `target_replica`: for each block c and generator replica g, the 4 quarters go to 4 different trainer replicas; for each block c and quarter k, the 4 generator replicas send to 4 different trainer replicas. `response_numbers`: never falls along a pack; every response number appears; a response has at most 3072 positions (rounded down), and one has exactly that many.
All inputs are finite; a program needn't handle non-finite values.
Results may differ from the reference program's by a relative error of at most 0.017.
Values may be sent and summed in bfloat16 or wider, within the bound.
No kernel may reach another device: no remote copies, remote signals or barrier semaphores. Data moves between devices by JAX's collectives and lax.ppermute only.
A program may use at most 128 MiB of HBM per device.

```python
import math
import jax
import jax.numpy as jnp
import numpy as np
from jax import lax

MODEL_WIDTH = 8192
HEAD_SIZE = 128
QUERY_HEADS = 32
KEY_VALUE_HEADS = 4
ADAPTER_RANK = 64
TOK_DEV = 128
DOCS = 4
REPLICA_COUNT = 4
SHARDS = 32
PACK_TOKENS = 4096


def draw_frozen_query(key, part):
    key = jax.random.fold_in(key, 11)
    query_shape = (REPLICA_COUNT, PACK_TOKENS, QUERY_HEADS * HEAD_SIZE)
    result = jnp.clip(jax.random.normal(jax.random.fold_in(key, 1), query_shape), -6.0, 6.0)
    return result.astype(jnp.bfloat16)


def draw_frozen_key_value(key, part):
    key = jax.random.fold_in(key, 12)
    key_shape = (REPLICA_COUNT, PACK_TOKENS, KEY_VALUE_HEADS * HEAD_SIZE)
    keys_part = jnp.clip(jax.random.normal(jax.random.fold_in(key, 1), key_shape), -6.0, 6.0)
    values_part = jnp.clip(jax.random.normal(jax.random.fold_in(key, 2), key_shape), -6.0, 6.0)
    return jnp.concatenate([keys_part, values_part], axis=-1).astype(jnp.bfloat16)


def draw_target_replica(key, part):
    key = jax.random.fold_in(key, 21)
    outer_keys = jax.random.split(jax.random.fold_in(key, 1), SHARDS)
    inner_keys = jax.random.split(jax.random.fold_in(key, 2), SHARDS)
    base = jnp.arange(REPLICA_COUNT, dtype=jnp.int32)
    outer = jax.vmap(lambda k: jax.random.permutation(k, base))(outer_keys)
    inner = jax.vmap(lambda k: jax.random.permutation(k, base))(inner_keys)
    slot = (inner[:, :, None] + base[None, None, :]) % REPLICA_COUNT
    flat_slot = slot.reshape(SHARDS, REPLICA_COUNT * REPLICA_COUNT)
    picked = jnp.take_along_axis(outer, flat_slot, axis=1)
    return picked.reshape(SHARDS, REPLICA_COUNT, REPLICA_COUNT).astype(jnp.int32)


def shard_levels(own_key, shape, cuts, least, top_value):
    gain = 1.0
    for axis_at, blocks in cuts:
        heights = jax.random.uniform(jax.random.fold_in(jax.random.fold_in(own_key, 6), axis_at), (blocks,), jnp.float32, least / len(cuts), top_value / len(cuts))
        gain = gain * jnp.repeat(jnp.exp(heights), shape[axis_at] // blocks).reshape((-1,) + (1,) * (len(shape) - 1 - axis_at))
    return gain


def profile(amount, total, bound, slope):
    loads = [(1 << 20) // math.isqrt(grade ** slope) + 1 for grade in range(2, amount + 1)]
    rest, given = total - bound - (amount - 1), [1] * (amount - 1)
    while rest > 0:
        movable = [i for i in range(amount - 1) if given[i] < bound]
        pool, budget = sum([loads[i] for i in movable]), rest
        for i in movable:
            more = min(bound - given[i], max(1, budget * loads[i] // pool), rest)
            given[i] = given[i] + more
            rest = rest - more
    return np.array([bound] + given)


def ragged(rng, amount, total, limit, lean):
    if amount == 2:
        one = jax.random.randint(rng, (), max(1, total - limit), min(limit, total - 1) + 1)
        return jnp.stack([one, total - one])
    tallies = jnp.asarray(profile(amount, total, limit, lean), jnp.int32)
    twos = (amount - 1) // 2
    donor, taker = tallies[1:1 + 2 * twos:2], tallies[2:2 + 2 * twos:2]
    room = jnp.minimum(donor - 1, limit - taker)
    moved = jax.random.randint(jax.random.fold_in(rng, 1), (twos,), 0, 1 << 20) % (room + 1)
    tallies = tallies.at[1:1 + 2 * twos:2].set(donor - moved).at[2:2 + 2 * twos:2].set(taker + moved)
    return tallies[jax.random.permutation(jax.random.fold_in(rng, 2), amount)]


def noise(rng, shape, deviation, reach, pieces=(), kind=jnp.bfloat16):
    values = deviation * jax.random.normal(rng, shape, jnp.float32)
    if pieces:
        values = values * shard_levels(rng, shape, pieces, -0.22, 0.18)
    return jnp.clip(values, -reach, reach).astype(kind)


def setup_inputs(seed: int = 0) -> dict:
    key_list = jax.random.split(jax.random.key(seed), 10)
    generated_input = noise(key_list[0], (REPLICA_COUNT, PACK_TOKENS, MODEL_WIDTH), 1.0, 6.0, ((0, 4), (1, 32)))
    frozen_query = draw_frozen_query(jax.random.fold_in(key_list[9], 71), 0)
    frozen_key_value = draw_frozen_key_value(jax.random.fold_in(key_list[9], 71), 0)
    adapter_down_weight = noise(key_list[3], (MODEL_WIDTH, 2 * ADAPTER_RANK), MODEL_WIDTH ** -0.5, 0.0625)
    query_up_weight = noise(key_list[4], (ADAPTER_RANK, QUERY_HEADS * HEAD_SIZE), ADAPTER_RANK ** -0.5, 0.75)
    value_up_weight = noise(key_list[5], (ADAPTER_RANK, KEY_VALUE_HEADS * HEAD_SIZE), ADAPTER_RANK ** -0.5, 0.75)
    response_numbers = jax.vmap(lambda own: jnp.searchsorted(jnp.cumsum(ragged(own, DOCS, PACK_TOKENS, 3 * PACK_TOKENS // 4, 1)), jnp.arange(PACK_TOKENS), side="right"))(jax.random.split(key_list[6], REPLICA_COUNT)).reshape((REPLICA_COUNT, PACK_TOKENS)).astype(jnp.int32)
    target_replica = draw_target_replica(jax.random.fold_in(key_list[9], 71), 0)
    output_gradient = noise(key_list[8], (REPLICA_COUNT, PACK_TOKENS, QUERY_HEADS * HEAD_SIZE), 1.0, 6.0, ((0, 4), (1, 32)))
    return dict(generated_input=generated_input, frozen_query=frozen_query, frozen_key_value=frozen_key_value, adapter_down_weight=adapter_down_weight, query_up_weight=query_up_weight, value_up_weight=value_up_weight, response_numbers=response_numbers, target_replica=target_replica, output_gradient=output_gradient)


ADAPTER_SCALE = 0.5

def to_low(values_in):
    return lax.optimization_barrier(values_in.astype(jnp.bfloat16)).astype(jnp.float32)

def attend(query_rows, key_row_block, value_rows, seg, output_cotangent):
    group_size = QUERY_HEADS // KEY_VALUE_HEADS
    inverse = 1.0 / math.sqrt(HEAD_SIZE)
    query_head_rows = query_rows.reshape(PACK_TOKENS, KEY_VALUE_HEADS, group_size, HEAD_SIZE).astype(jnp.float32)
    key_head_rows = key_row_block.reshape(PACK_TOKENS, KEY_VALUE_HEADS, HEAD_SIZE).astype(jnp.float32)
    value_head_rows = value_rows.reshape(PACK_TOKENS, KEY_VALUE_HEADS, HEAD_SIZE).astype(jnp.float32)
    head_gradients = output_cotangent.reshape(PACK_TOKENS, KEY_VALUE_HEADS, group_size, HEAD_SIZE).astype(jnp.float32)
    block_length = math.gcd(PACK_TOKENS, 512)
    columns = jnp.arange(PACK_TOKENS, dtype=jnp.int32)

    def single_block(value_gradient, step_index):
        first_row = step_index * block_length
        q_block = lax.dynamic_slice_in_dim(query_head_rows, first_row, block_length, 0)
        g_block = lax.dynamic_slice_in_dim(head_gradients, first_row, block_length, 0)
        seg_block = lax.dynamic_slice_in_dim(seg, first_row, block_length, 0)
        positions = first_row + jnp.arange(block_length, dtype=jnp.int32)
        visible = (seg_block[:, None] == seg[None, :]) & (columns[None, :] <= positions[:, None])
        raw_scores = jnp.einsum('rkgd,tkd->kgrt', q_block, key_head_rows) * inverse
        masked = jnp.where(visible, raw_scores, -jnp.inf)
        row_max = lax.optimization_barrier(jnp.max(masked, axis=-1, keepdims=True))
        weight = jnp.exp(masked - row_max)
        row_sum = lax.optimization_barrier(jnp.sum(weight, axis=-1, keepdims=True))
        output = jnp.einsum('kgrt,tkd->rkgd', to_low(weight), value_head_rows) / jnp.transpose(row_sum, (2, 0, 1, 3))
        out_low = output.astype(jnp.bfloat16)
        log_total = row_max + jnp.log(row_sum)
        prob_rows = jnp.exp(masked - log_total)
        prob_grad = jnp.einsum('rkgd,tkd->kgrt', g_block, value_head_rows)
        row_delta = jnp.transpose(lax.optimization_barrier(jnp.sum(g_block * to_low(output), axis=-1)), (1, 2, 0))[..., None]
        score_grad = to_low(prob_rows * (prob_grad - row_delta))
        q_grad = jnp.einsum('kgrt,tkd->rkgd', score_grad, key_head_rows) * inverse
        value_gradient = value_gradient + jnp.einsum('kgrt,rkgd->tkd', to_low(prob_rows), g_block)
        return (value_gradient, (out_low, q_grad.astype(jnp.bfloat16)))
    value_gradient, (output_list, query_gradients) = lax.scan(single_block, jnp.zeros((PACK_TOKENS, KEY_VALUE_HEADS, HEAD_SIZE), jnp.float32), jnp.arange(PACK_TOKENS // block_length, dtype=jnp.int32))
    return (output_list.reshape(PACK_TOKENS, QUERY_HEADS * HEAD_SIZE), query_gradients.reshape(PACK_TOKENS, QUERY_HEADS * HEAD_SIZE), value_gradient.reshape(PACK_TOKENS, KEY_VALUE_HEADS * HEAD_SIZE))

def regroup(stacked, chooser):
    quarter_len = TOK_DEV // REPLICA_COUNT
    width = stacked.shape[-1]
    blocks = stacked.reshape(REPLICA_COUNT, SHARDS, REPLICA_COUNT, quarter_len, width)
    wide_index = jnp.broadcast_to(chooser[:, :, :, None, None].astype(jnp.int32), blocks.shape)
    picked = jnp.take_along_axis(blocks, wide_index, axis=0)
    return picked.reshape(REPLICA_COUNT, PACK_TOKENS, width)

def attend_packed(packed):
    return attend(packed[0], packed[1], packed[2], packed[3], packed[4])

def reference(generated_input, frozen_query, frozen_key_value, adapter_down_weight, query_up_weight, value_up_weight, response_numbers, target_replica, output_gradient):
    key_value_width = KEY_VALUE_HEADS * HEAD_SIZE
    highest_precision = lax.Precision.HIGHEST
    flattened_input = generated_input.reshape(REPLICA_COUNT * PACK_TOKENS, MODEL_WIDTH)
    reduced_rows = jnp.dot(flattened_input, adapter_down_weight, preferred_element_type=jnp.float32).astype(jnp.bfloat16)
    reduced_rows = reduced_rows.reshape(REPLICA_COUNT, PACK_TOKENS, 2 * ADAPTER_RANK)
    places = jnp.arange(REPLICA_COUNT, dtype=jnp.int32)
    match = (target_replica[:, None, :, :] == places[None, :, None, None]).astype(jnp.int32)
    source = lax.optimization_barrier(jnp.sum(places[None, None, :, None] * match, axis=2)).astype(jnp.int32)
    forward_pick = jnp.transpose(source, (1, 0, 2))
    query_input = regroup(frozen_query, forward_pick)
    key_value_input = regroup(frozen_key_value, forward_pick)
    reduced_input = regroup(reduced_rows, forward_pick)
    reduced_query = reduced_input[:, :, :ADAPTER_RANK].astype(jnp.float32)
    reduced_value = reduced_input[:, :, ADAPTER_RANK:].astype(jnp.float32)
    query_rows = (query_input.astype(jnp.float32) + ADAPTER_SCALE * jnp.einsum('vqj,je->vqe', reduced_query, query_up_weight.astype(jnp.float32))).astype(jnp.bfloat16)
    key_row_block = key_value_input[:, :, :key_value_width]
    value_rows = (key_value_input[:, :, key_value_width:].astype(jnp.float32) + ADAPTER_SCALE * jnp.einsum('vqj,je->vqe', reduced_value, value_up_weight.astype(jnp.float32))).astype(jnp.bfloat16)
    attn_out, q_grad, v_grad = lax.map(attend_packed, (query_rows, key_row_block, value_rows, response_numbers, output_gradient))
    query_gradient32 = q_grad.astype(jnp.float32)
    value_gradient32 = v_grad.astype(jnp.float32)
    query_up_gradient = ADAPTER_SCALE * jnp.einsum('sdb,sdh->bh', reduced_query, query_gradient32)
    value_up_gradient = ADAPTER_SCALE * jnp.einsum('sdb,sdh->bh', reduced_value, value_gradient32, precision=highest_precision)
    reduced_gradient = jnp.concatenate([ADAPTER_SCALE * jnp.einsum('pcx,qx->pcq', query_gradient32, query_up_weight.astype(jnp.float32)), ADAPTER_SCALE * jnp.einsum('pcx,qx->pcq', value_gradient32, value_up_weight.astype(jnp.float32), precision=highest_precision)], axis=-1).astype(jnp.bfloat16)
    low_back = regroup(reduced_gradient, jnp.transpose(target_replica, (1, 0, 2)))
    grad_a = jnp.dot(jnp.transpose(flattened_input), low_back.reshape(REPLICA_COUNT * PACK_TOKENS, 2 * ADAPTER_RANK), preferred_element_type=jnp.float32)
    return (attn_out, grad_a, query_up_gradient, value_up_gradient)
```

```python
import functools
import math

import jax
import jax.numpy as jnp
from jax import lax
from jax.experimental import pallas as pl
from jax.experimental.pallas import tpu as pltpu
from jax.sharding import Mesh
from jax.sharding import PartitionSpec as P

HEAD = 128
BLOCK = 128
QUARTER = 32
KEY_CHUNK = 512
PAD = KEY_CHUNK - BLOCK
HEADS_STEP = 4
SCALE = 0.5
MASKED = -1e30
INVERSE = 1.0 / math.sqrt(HEAD)
LOG2E = 1.4426950408889634
BF = jnp.bfloat16
F32 = jnp.float32
NT = (((1,), (1,)), ((), ()))
TN = (((0,), (0,)), ((), ()))
VMEM = pltpu.VMEM
CHIP = ("dp", "y", "x")
LANE = ("x", "core")


def whole():
    return pl.BlockSpec(memory_space=pltpu.VMEM)


def scalars():
    return pl.BlockSpec(memory_space=pltpu.SMEM)


def params(mib):
    return pltpu.CompilerParams(vmem_limit_bytes=mib << 20)


def front_kernel(order_ref, x_ref, a_ref, kv_ref, out_ref, low_ref):
    low_ref[...] = jnp.dot(x_ref[...], a_ref[...], preferred_element_type=F32).astype(BF)
    for r in range(4):
        rows = pl.ds(pl.multiple_of(order_ref[r] * QUARTER, QUARTER), QUARTER)
        low = low_ref[rows, :]
        for y in range(4):
            out_ref[r * 4 + y, :, 0:128] = kv_ref[rows, y * 128 : y * 128 + 128]
            out_ref[r * 4 + y, :, 128:256] = kv_ref[rows, 512 + y * 128 : 640 + y * 128]
            out_ref[r * 4 + y, :, 256:384] = low


def front(order, x, a, kv):
    return pl.pallas_call(
        front_kernel,
        out_shape=jax.ShapeDtypeStruct((16, QUARTER, 384), BF),
        in_specs=[scalars(), whole(), whole(), whole()],
        out_specs=whole(),
        scratch_shapes=[VMEM((BLOCK, 128), BF)],
        compiler_params=params(32),
        cost_estimate=pl.CostEstimate(flops=2 * 128 * 8192 * 128, bytes_accessed=5 << 20, transcendentals=0),
    )(order, x, a, kv)


def query_chunks_kernel(order_ref, q_ref, out_ref):
    for y in range(4):
        out_ref[0, y] = q_ref[:, y * 1024 : (y + 1) * 1024]


def query_chunks(order, q):
    return pl.pallas_call(
        query_chunks_kernel,
        out_shape=jax.ShapeDtypeStruct((4, 4, QUARTER, 1024), BF),
        grid_spec=pltpu.PrefetchScalarGridSpec(
            num_scalar_prefetch=1,
            grid=(4,),
            in_specs=[pl.BlockSpec((QUARTER, 4096), lambda r, order: (order[r], 0))],
            out_specs=pl.BlockSpec((1, 4, QUARTER, 1024), lambda r, order: (r, 0, 0, 0)),
        ),
        cost_estimate=pl.CostEstimate(flops=0, bytes_accessed=2 << 20, transcendentals=0),
    )(order, q)


def pack_kernel(order_ref, c0, c1, c2, c3, resp_ref, wv_ref, out_ref):
    rows = jnp.concatenate([c0[0], c1[0], c2[0], c3[0]], axis=0)
    low_v = rows[:, 320:384]
    value = rows[:, 128:256].astype(F32) + SCALE * jnp.dot(low_v, wv_ref[...], preferred_element_type=F32)
    lane = lax.broadcasted_iota(jnp.int32, (BLOCK, 64), 1)
    resp = resp_ref[0].astype(F32)
    extra = jnp.where(lane == 0, 1.0, jnp.where(lane == 1, resp, 0.0))
    out_ref[0, :, 0:128] = rows[:, 0:128]
    out_ref[0, :, 128:256] = value.astype(BF)
    out_ref[0, :, 256:384] = jnp.concatenate([low_v.astype(F32), extra], axis=1).astype(BF)


def pack(order, got, resp, wv):
    def chunk(k):
        return pl.BlockSpec((1, QUARTER, 384), lambda i, order: (order[i * 4 + k], 0, 0))

    return pl.pallas_call(
        pack_kernel,
        out_shape=jax.ShapeDtypeStruct((4, BLOCK, 384), BF),
        grid_spec=pltpu.PrefetchScalarGridSpec(
            num_scalar_prefetch=1,
            grid=(4,),
            in_specs=[chunk(k) for k in range(4)]
            + [
                pl.BlockSpec((1, BLOCK, 1), lambda i, order: (i, 0, 0)),
                pl.BlockSpec((64, 128), lambda i, order: (0, 0)),
            ],
            out_specs=pl.BlockSpec((1, BLOCK, 384), lambda i, order: (i, 0, 0)),
        ),
        cost_estimate=pl.CostEstimate(flops=1 << 23, bytes_accessed=1 << 20, transcendentals=0),
    )(order, got, got, got, got, resp, wv)


def attention_kernel(
    order_ref, steps_ref, lane_ref,
    q0, q1, q2, q3, l0, l1, l2, l3, do_ref, start_ref, kv_ref, wv_ref, wq_ref,
    out_ref, lg_ref, send_ref,
    kv_s, s_s, w_s, t_s, m_s, acc_s, dq_s, qup_s, vup_s, sem,
):
    i, hg = pl.program_id(0), pl.program_id(1)
    rows_all = HEADS_STEP * BLOCK

    @pl.when((i == 0) & (hg == 0))
    def _():
        copies = []
        for c in range(32):
            copies.append(
                pltpu.make_async_copy(
                    kv_ref.at[c % 8, c // 8], kv_s.at[pl.ds(PAD + c * BLOCK, BLOCK), :], sem.at[c]
                )
            )
        for copy in copies:
            copy.start()
        kv_s[0:PAD, :] = jnp.zeros((PAD, 384), BF)
        t_s[...] = jnp.zeros_like(t_s)
        qup_s[...] = jnp.zeros_like(qup_s)
        vup_s[...] = jnp.zeros_like(vup_s)
        for copy in copies:
            copy.wait()

    @pl.when(hg == 0)
    def _():
        lg_ref[...] = jnp.zeros_like(lg_ref)

    block = i * 8 + lane_ref[0]
    high = (block + 1) * BLOCK
    steps = steps_ref[i]

    low = jnp.concatenate([l0[0], l1[0], l2[0], l3[0]], axis=0)
    wq = wq_ref[...]
    q_in = jnp.concatenate([q0[0], q1[0], q2[0], q3[0]], axis=0).astype(F32)
    query = (q_in + SCALE * jnp.dot(low[:, 0:64], wq, preferred_element_type=F32)).astype(BF)
    query = jnp.concatenate([query[:, h * HEAD : (h + 1) * HEAD] for h in range(HEADS_STEP)], axis=0)
    dout = do_ref[0]
    dout = jnp.concatenate([dout[:, h * HEAD : (h + 1) * HEAD] for h in range(HEADS_STEP)], axis=0)
    start = jnp.concatenate([start_ref[0]] * HEADS_STEP, axis=0)
    row = block * BLOCK + lax.broadcasted_iota(jnp.int32, (BLOCK, 1), 0)
    row = jnp.concatenate([row] * HEADS_STEP, axis=0)

    def place(t):
        return pl.multiple_of(PAD + high - KEY_CHUNK * (t + 1), BLOCK)

    m_s[...] = jnp.full_like(m_s, MASKED)

    def scores(t, _):
        at = place(t)
        s = lax.dot_general(query, kv_s[pl.ds(at, KEY_CHUNK), 0:128], NT, preferred_element_type=F32)
        key = at - PAD + lax.broadcasted_iota(jnp.int32, (1, KEY_CHUNK), 1)
        s = jnp.where((key >= start) & (key <= row), s, MASKED)
        s_s[t] = s
        top = m_s[...]
        for c in range(KEY_CHUNK // 128):
            top = jnp.maximum(top, s[:, c * 128 : (c + 1) * 128])
        m_s[...] = top
        return 0

    lax.fori_loop(0, steps, scores, 0)
    top = jnp.max(m_s[...], axis=1, keepdims=True)
    acc_s[...] = jnp.zeros_like(acc_s)

    def forward(t, _):
        w = jnp.exp2((s_s[t] - top) * (INVERSE * LOG2E)).astype(BF)
        w_s[t] = w
        acc_s[...] += jnp.dot(w, kv_s[pl.ds(place(t), KEY_CHUNK), 128:384], preferred_element_type=F32)
        return 0

    lax.fori_loop(0, steps, forward, 0)
    over = 1.0 / acc_s[:, 192:193]
    out = (acc_s[:, 0:128] * over).astype(BF)
    for h in range(HEADS_STEP):
        out_ref[0, :, h * HEAD : (h + 1) * HEAD] = out[h * BLOCK : (h + 1) * BLOCK, :]
    wide = dout.astype(F32)
    delta = jnp.sum(wide * out.astype(F32), axis=1, keepdims=True) * over
    scaled = (wide * over).astype(BF)
    g = lax.dot_general(wv_ref[...], scaled, NT, preferred_element_type=F32).astype(BF)
    weighted_low = (acc_s[:, 128:256] * over).astype(BF)
    vup_s[...] += lax.dot_general(weighted_low, dout, TN, preferred_element_type=F32)
    dq_s[...] = jnp.zeros_like(dq_s)

    def backward(t, _):
        at = place(t)
        w = w_s[t]
        dp = lax.dot_general(scaled, kv_s[pl.ds(at, KEY_CHUNK), 128:256], NT, preferred_element_type=F32)
        ds = (w.astype(F32) * (dp - delta)).astype(BF)
        dq_s[...] += jnp.dot(ds, kv_s[pl.ds(at, KEY_CHUNK), 0:128], preferred_element_type=F32)
        t_s[:, pl.ds(at, KEY_CHUNK)] += jnp.dot(g, w, preferred_element_type=F32)
        return 0

    lax.fori_loop(0, steps, backward, 0)
    dq = (dq_s[...] * INVERSE).astype(BF)
    low_t = jnp.transpose(low.astype(F32))[0:64, :].astype(BF)
    lg = lg_ref[...]
    for h in range(HEADS_STEP):
        dq_h = dq[h * BLOCK : (h + 1) * BLOCK, :]
        lg = lg + lax.dot_general(
            wq[:, h * HEAD : (h + 1) * HEAD], dq_h, NT, preferred_element_type=F32
        )
        qup_s[hg * HEADS_STEP + h] += jnp.dot(low_t, dq_h, preferred_element_type=F32)
    lg_ref[...] = lg

    @pl.when((i == 3) & (hg == 8 // HEADS_STEP - 1))
    def _():
        for c in range(32):
            part = t_s[:, PAD + c * BLOCK : PAD + (c + 1) * BLOCK] * SCALE
            send_ref[c % 8, :, (c // 8) * BLOCK : (c // 8 + 1) * BLOCK] = part.astype(BF)
        vup = (vup_s[0:64, :] * SCALE).astype(BF)
        for c in range(8):
            send_ref[c, :, 512:640] = (qup_s[c] * SCALE).astype(BF)
            send_ref[c, :, 640:768] = vup


def attention(order, steps, lane, q, got, dout, start, kv, wv, wq):
    width = HEADS_STEP * HEAD
    rows = HEADS_STEP * BLOCK
    chunks = 4096 // KEY_CHUNK

    def q_part(k):
        return pl.BlockSpec((1, QUARTER, width), lambda i, h, order, *_: (order[i * 4 + k], 0, h))

    def low_part(k):
        return pl.BlockSpec((1, QUARTER, 128), lambda i, h, order, *_: (order[i * 4 + k], 0, 2))

    return pl.pallas_call(
        attention_kernel,
        out_shape=(
            jax.ShapeDtypeStruct((4, BLOCK, 1024), BF),
            jax.ShapeDtypeStruct((64, 512), F32),
            jax.ShapeDtypeStruct((8, 64, 768), BF),
        ),
        grid_spec=pltpu.PrefetchScalarGridSpec(
            num_scalar_prefetch=3,
            grid=(4, 8 // HEADS_STEP),
            in_specs=[q_part(k) for k in range(4)]
            + [low_part(k) for k in range(4)]
            + [
                pl.BlockSpec((1, BLOCK, width), lambda i, h, *_: (i, 0, h)),
                pl.BlockSpec((1, BLOCK, 1), lambda i, h, *_: (i, 0, 0)),
                pl.BlockSpec(memory_space=pl.ANY),
                pl.BlockSpec((64, 128), lambda i, h, *_: (0, 0)),
                pl.BlockSpec((64, width), lambda i, h, *_: (0, h)),
            ],
            out_specs=(
                pl.BlockSpec((1, BLOCK, width), lambda i, h, *_: (i, 0, h)),
                pl.BlockSpec((64, BLOCK), lambda i, h, *_: (0, i)),
                pl.BlockSpec((8, 64, 768), lambda i, h, *_: (0, 0, 0)),
            ),
            scratch_shapes=[
                VMEM((PAD + 4096, 384), BF),
                VMEM((chunks, rows, KEY_CHUNK), F32),
                VMEM((chunks, rows, KEY_CHUNK), BF),
                VMEM((64, PAD + 4096), F32),
                VMEM((rows, 128), F32),
                VMEM((rows, 256), F32),
                VMEM((rows, 128), F32),
                VMEM((8, 64, 128), F32),
                VMEM((128, 128), F32),
                pltpu.SemaphoreType.DMA((32,)),
            ],
        ),
        compiler_params=params(48),
        cost_estimate=pl.CostEstimate(flops=20 << 30, bytes_accessed=8 << 20, transcendentals=8 << 20),
    )(order, steps, lane, q, q, q, q, got, got, got, got, dout, start, kv, wv, wq)


def middle_kernel(back_ref, mine_ref, got_ref, lg_ref, out_ref, low_ref):
    total = got_ref[0].astype(F32)
    for c in range(1, 8):
        total = total + got_ref[c].astype(F32)
    low_ref[...] = jnp.transpose(jnp.concatenate([lg_ref[...] * SCALE, total[:, 0:512]], axis=0))
    for g in range(4):
        for y in range(4):
            rows = pl.ds(pl.multiple_of(y * BLOCK + back_ref[g * 4 + y] * QUARTER, QUARTER), QUARTER)
            out_ref[g * 4 + y, 0:32, :] = low_ref[rows, :].astype(BF)
            keep = jnp.where(mine_ref[0] == y, 1.0, 0.0)
            out_ref[g * 4 + y, 32:48, :] = (total[g * 16 : g * 16 + 16, 512:640] * keep).astype(BF)
            out_ref[g * 4 + y, 48:64, :] = (total[g * 16 : g * 16 + 16, 640:768] * keep).astype(BF)


def middle(back, mine, got, lg):
    return pl.pallas_call(
        middle_kernel,
        out_shape=jax.ShapeDtypeStruct((16, 64, 128), BF),
        in_specs=[scalars(), scalars(), whole(), whole()],
        out_specs=whole(),
        scratch_shapes=[VMEM((512, 128), F32)],
        cost_estimate=pl.CostEstimate(flops=1 << 20, bytes_accessed=1 << 20, transcendentals=0),
    )(back, mine, got, lg)


def low_back_kernel(outgoing_ref, got_ref, low_ref, up_ref, sum_ref):
    up = jnp.zeros((32, 128), F32)
    for r in range(4):
        total = got_ref[r * 4].astype(F32)
        for y in range(1, 4):
            total = total + got_ref[r * 4 + y].astype(F32)
        sum_ref[r] = total[0:32, :]
        up = up + total[32:64, :]
    for k in range(4):
        low_ref[k * QUARTER : (k + 1) * QUARTER, :] = sum_ref[outgoing_ref[k]].astype(BF)
    up_ref[...] = up


def low_back_of(outgoing, got):
    return pl.pallas_call(
        low_back_kernel,
        out_shape=(jax.ShapeDtypeStruct((BLOCK, 128), BF), jax.ShapeDtypeStruct((32, 128), F32)),
        in_specs=[scalars(), whole()],
        out_specs=(whole(), whole()),
        scratch_shapes=[VMEM((4, QUARTER, 128), F32)],
        cost_estimate=pl.CostEstimate(flops=1 << 18, bytes_accessed=1 << 19, transcendentals=0),
    )(outgoing, got)


def on_device(
    generated_input,
    frozen_query,
    frozen_key_value,
    adapter_down_weight,
    query_up_weight,
    value_up_weight,
    response_numbers,
    target_replica,
    output_gradient,
):
    me = lax.axis_index("dp")
    my_y = lax.axis_index("y")
    my_core = lax.axis_index("core")
    my_lane = lax.axis_index("x") * 2 + my_core
    places = jnp.arange(4, dtype=jnp.int32)
    route = target_replica[0]
    outgoing = lax.dynamic_index_in_dim(route, me, 0, keepdims=False)
    send_order = jnp.sum(places[None, :] * (outgoing[None, :] == places[:, None]), axis=1).astype(jnp.int32)
    swap = [(0, 1), (1, 0)]

    rows = generated_input[0]
    own_half = lax.dynamic_slice_in_dim(rows, my_core * 4096, 4096, 1)
    other_half = lax.ppermute(
        lax.dynamic_slice_in_dim(rows, (1 - my_core) * 4096, 4096, 1), "core", swap
    )

    notes = jnp.concatenate([response_numbers[0], route.reshape(16), jnp.zeros((112,), jnp.int32)])
    notes = lax.all_to_all(jnp.broadcast_to(notes.reshape(1, 2, 128), (4, 2, 128)), "y", 0, 0, tiled=True)
    resp = notes[:, 0, :]
    routes = notes[:, 1, 0:16].reshape(4, 4, 4)
    mine = (routes == me).astype(jnp.int32)
    order = (jnp.sum(mine * places[None, :, None], axis=1) * 4 + places[:, None]).reshape(16)
    back = jnp.transpose(jnp.sum(mine * places[None, None, :], axis=2)).reshape(16)

    got = lax.all_to_all(
        front(send_order, rows, adapter_down_weight, frozen_key_value[0]), ("dp", "y"), 0, 0, tiled=True
    )
    wv = lax.dynamic_slice_in_dim(value_up_weight, my_y * 128, 128, 1)
    wq = lax.dynamic_slice_in_dim(query_up_weight, my_y * 1024, 1024, 1)
    packed = pack(order, got, resp[:, :, None], wv)
    kv = lax.all_gather(packed, LANE, axis=0, tiled=False)
    q = lax.all_to_all(
        query_chunks(send_order, frozen_query[0]).reshape(16, QUARTER, 1024), ("dp", "y"), 0, 0, tiled=True
    )
    dout = lax.all_to_all(
        jnp.transpose(output_gradient[0].reshape(BLOCK, 4, 1024), (1, 0, 2)), "y", 0, 0, tiled=True
    )

    all_resp = kv[:, :, :, 321].astype(jnp.int32)
    below = jnp.sum(all_resp.reshape(1, -1) < places[:, None], axis=1).astype(jnp.int32)
    start = jnp.sum((resp[:, :, None] == places) * below, axis=2).astype(jnp.int32)
    high = ((places * 8 + my_lane) + 1) * BLOCK
    steps = (high - start[:, 0] + KEY_CHUNK - 1) // KEY_CHUNK

    out, lg, send = attention(
        order, steps, my_lane.reshape(1), q, got, dout, start[:, :, None], kv, wv, wq
    )
    sums = lax.all_to_all(send, LANE, 0, 0, tiled=True)
    chunks = lax.all_to_all(middle(back, my_y.reshape(1), sums, lg), ("dp", "y"), 0, 0, tiled=True)
    low_back, up = low_back_of(outgoing, chunks)
    low_other = lax.ppermute(low_back, "core", swap)
    grad = lax.dot_general(
        jnp.concatenate([own_half, other_half], axis=0),
        jnp.concatenate([low_back, low_other], axis=0),
        TN,
        preferred_element_type=F32,
    ).astype(BF)
    parts = lax.all_to_all(grad.reshape(64, 64, 128), CHIP, 0, 0, tiled=True)
    grad_rows = jnp.sum(parts.astype(F32), axis=0)
    vup_rows = lax.dynamic_slice_in_dim(up[16:32], my_lane * 2, 2, 0)
    shard = jnp.concatenate([grad_rows, up[0:16], vup_rows, jnp.zeros((6, 128), F32)], axis=0).astype(BF)
    own = lax.all_to_all(jnp.broadcast_to(shard[None], (64, 88, 128)), CHIP, 0, 0, tiled=True)
    other = lax.ppermute(own, "core", swap)
    first = jnp.where(my_core == 0, own, other)
    second = jnp.where(my_core == 0, other, own)
    both = jnp.stack([first, second], axis=1)
    grad_a = jnp.transpose(both[:, :, 0:64], (1, 0, 2, 3)).reshape(8192, 128).astype(F32)
    both = both.reshape(4, 4, 8, 88, 128)
    query_up_gradient = jnp.transpose(both[:, :, :, 64:80], (0, 3, 1, 2, 4)).reshape(64, 4096).astype(F32)
    value_up_gradient = jnp.transpose(both[:, :, :, 80:82], (0, 2, 3, 1, 4)).reshape(64, 512).astype(F32)

    out = lax.all_to_all(out, "y", 0, 0, tiled=True)
    attn_out = jnp.transpose(out, (1, 0, 2)).reshape(1, BLOCK, 4096)
    return (attn_out, grad_a, query_up_gradient, value_up_gradient)


def solution(mesh):
    grid = Mesh(mesh.devices.reshape(4, 4, 4, 2), ("dp", "y", "x", "core"))
    ctx = ("y", "x", "core")
    return jax.shard_map(
        on_device,
        mesh=grid,
        in_specs=(
            P("dp", ctx, None),
            P("dp", ctx, None),
            P("dp", ctx, None),
            P(),
            P(),
            P(),
            P("dp", ctx),
            P(ctx, None, None),
            P("dp", ctx, None),
        ),
        out_specs=(P("dp", ctx, None), P(), P(), P()),
        check_vma=False,
    )
```

```python
import functools
import math

import jax
import jax.numpy as jnp
from jax import lax
from jax.experimental import pallas as pl
from jax.experimental.pallas import tpu as pltpu
from jax.sharding import Mesh
from jax.sharding import PartitionSpec as P

HEAD = 128
BLOCK = 128
QUARTER = 32
KEY_CHUNK = 512
PAD = KEY_CHUNK - BLOCK
ROWS_STEP = 8 * BLOCK
SCALE = 0.5
MASKED = -1e30
INVERSE = 1.0 / math.sqrt(HEAD)
LOG2E = 1.4426950408889634
BF = jnp.bfloat16
F32 = jnp.float32
NT = (((1,), (1,)), ((), ()))
TN = (((0,), (0,)), ((), ()))
VMEM = pltpu.VMEM
CHIP = ("dp", "y", "x")
ROWS = ("dp", "y")
ALL = ("dp", "y", "x", "core")
SHARD = 88


def turn(d):
    return [(y, (y + d) % 4) for y in range(4)]


def whole():
    return pl.BlockSpec(memory_space=pltpu.VMEM)


def scalars():
    return pl.BlockSpec(memory_space=pltpu.SMEM)


def params(mib):
    return pltpu.CompilerParams(vmem_limit_bytes=mib << 20)


def front_kernel(order_ref, x_ref, a_ref, kv_ref, out_ref, acc_ref, low_ref):
    step = pl.program_id(0)

    @pl.when(step == 0)
    def _():
        acc_ref[...] = jnp.zeros_like(acc_ref)

    acc_ref[...] += jnp.dot(x_ref[...], a_ref[...], preferred_element_type=F32)

    @pl.when(step == pl.num_programs(0) - 1)
    def _():
        low_ref[...] = acc_ref[...].astype(BF)
        for r in range(4):
            rows = pl.ds(pl.multiple_of(order_ref[r] * QUARTER, QUARTER), QUARTER)
            low = low_ref[rows, :]
            for y in range(4):
                out_ref[r * 4 + y, :, 0:128] = kv_ref[rows, y * 128 : y * 128 + 128]
                out_ref[r * 4 + y, :, 128:256] = kv_ref[rows, 512 + y * 128 : 640 + y * 128]
                out_ref[r * 4 + y, :, 256:384] = low


def front(order, x, a, kv):
    steps = 8
    part = 8192 // steps
    return pl.pallas_call(
        front_kernel,
        out_shape=jax.ShapeDtypeStruct((16, QUARTER, 384), BF),
        grid_spec=pltpu.PrefetchScalarGridSpec(
            num_scalar_prefetch=1,
            grid=(steps,),
            in_specs=[
                pl.BlockSpec((BLOCK, part), lambda i, order: (0, i)),
                pl.BlockSpec((part, 128), lambda i, order: (i, 0)),
                pl.BlockSpec((BLOCK, 1024), lambda i, order: (0, 0)),
            ],
            out_specs=pl.BlockSpec((16, QUARTER, 384), lambda i, order: (0, 0, 0)),
            scratch_shapes=[VMEM((BLOCK, 128), F32), VMEM((BLOCK, 128), BF)],
        ),
        compiler_params=params(58),
        cost_estimate=pl.CostEstimate(flops=2 * 128 * 8192 * 128, bytes_accessed=5 << 20, transcendentals=0),
    )(order, x, a, kv)


def query_chunks_kernel(order_ref, q_ref, out_ref, sem):
    copies = []
    for r in range(4):
        rows = pl.ds(pl.multiple_of(order_ref[r] * QUARTER, QUARTER), QUARTER)
        for y in range(4):
            copies.append(
                pltpu.make_async_copy(
                    q_ref.at[rows, pl.ds(y * 1024, 1024)], out_ref.at[r * 4 + y], sem.at[r * 4 + y]
                )
            )
    for copy in copies:
        copy.start()
    for copy in copies:
        copy.wait()


def query_chunks(order, q):
    return pl.pallas_call(
        query_chunks_kernel,
        out_shape=jax.ShapeDtypeStruct((16, QUARTER, 1024), BF),
        in_specs=[scalars(), pl.BlockSpec(memory_space=pl.ANY)],
        out_specs=pl.BlockSpec(memory_space=pl.ANY),
        scratch_shapes=[pltpu.SemaphoreType.DMA((16,))],
        compiler_params=params(48),
        cost_estimate=pl.CostEstimate(flops=0, bytes_accessed=2 << 20, transcendentals=0),
    )(order, q)


def pack_kernel(scalar_ref, got_ref, notes_ref, wv_ref, out_ref):
    lane = lax.broadcasted_iota(jnp.int32, (QUARTER, 64), 1)
    for i in range(4):
        y = scalar_ref[28 + i]
        below = [
            jnp.sum(jnp.where(notes_ref[i, 0:1, :] < v, 1.0, 0.0), axis=1, keepdims=True) for v in range(1, 4)
        ]
        for k in range(4):
            at = scalar_ref[i * 4 + k]
            rows = got_ref[at]
            low_v = rows[:, 320:384]
            value = rows[:, 128:256].astype(F32) + SCALE * jnp.dot(
                low_v, wv_ref[...], preferred_element_type=F32
            )
            source = (at // 4).astype(F32)
            extra = jnp.where(lane == 0, 1.0, jnp.where(lane == 1, source, 0.0))
            for v in range(1, 4):
                extra = jnp.where(lane == 1 + v, below[v - 1], extra)
            span = slice(k * QUARTER, (k + 1) * QUARTER)
            out_ref[y, span, 0:128] = rows[:, 0:128]
            out_ref[y, span, 128:256] = value.astype(BF)
            out_ref[y, span, 256:384] = jnp.concatenate([low_v.astype(F32), extra], axis=1).astype(BF)


def pack(scalar, got, notes, wv):
    return pl.pallas_call(
        pack_kernel,
        out_shape=jax.ShapeDtypeStruct((4, BLOCK, 384), BF),
        in_specs=[scalars(), whole(), whole(), whole()],
        out_specs=whole(),
        cost_estimate=pl.CostEstimate(flops=1 << 23, bytes_accessed=1 << 20, transcendentals=0),
    )(scalar, got, notes, wv)


def attention_kernel(
    scalar_ref, q_ref, got_ref, d0, d1, d2, d3, notes_ref, kv_ref, wv_ref, wq_ref,
    out_ref, send_ref, up_ref,
    kv_s, s_s, w_s, t_s, m_s, acc_s, dq_s, dout_s, lg_s, qup_s, vup_s, below_s, sem,
):
    copies = []
    for c in range(32):
        copies.append(
            pltpu.make_async_copy(
                kv_ref.at[c % 8, c // 8], kv_s.at[pl.ds(PAD + c * BLOCK, BLOCK), :], sem.at[c]
            )
        )
    for copy in copies:
        copy.start()
    kv_s[0:PAD, :] = jnp.zeros((PAD, 384), BF)
    t_s[...] = jnp.zeros_like(t_s)
    qup_s[...] = jnp.zeros_like(qup_s)
    vup_s[...] = jnp.zeros_like(vup_s)
    for i, d in enumerate((d0, d1, d2, d3)):
        for h in range(8):
            dout_s[i, h * BLOCK : (h + 1) * BLOCK, :] = d[:, h * HEAD : (h + 1) * HEAD]
    for copy in copies:
        copy.wait()
    counts = kv_s[PAD : PAD + 16, 256:384].astype(F32)
    for c in range(1, 32):
        counts = counts + kv_s[PAD + c * BLOCK : PAD + c * BLOCK + 16, 256:384].astype(F32)
    lane = lax.broadcasted_iota(jnp.int32, (1, 128), 1)
    below_s[0] = 0
    for v in range(1, 4):
        below_s[v] = jnp.sum(jnp.where(lane == 65 + v, counts[0:1, :], 0.0)).astype(jnp.int32)
    diagonal = lax.broadcasted_iota(jnp.int32, (BLOCK, BLOCK), 0) == lax.broadcasted_iota(
        jnp.int32, (BLOCK, BLOCK), 1
    )

    def turn_of(i, _):
        block = scalar_ref[16 + i]
        high = (block + 1) * BLOCK
        steps = (high - below_s[scalar_ref[20 + i]] + KEY_CHUNK - 1) // KEY_CHUNK
        clean = jnp.clip((high - below_s[scalar_ref[24 + i]]) // KEY_CHUNK, 1, steps)
        resp = notes_ref[i, 0:1, :]
        start = jnp.zeros((1, BLOCK), jnp.int32)
        for v in range(1, 4):
            start = jnp.where(resp == v, below_s[v], start)
        start = jnp.sum(jnp.where(diagonal, start.astype(F32), 0.0), axis=1, keepdims=True).astype(jnp.int32)
        start = jnp.concatenate([start] * 8, axis=0)
        row = block * BLOCK + lax.broadcasted_iota(jnp.int32, (BLOCK, 1), 0)
        row = jnp.concatenate([row] * 8, axis=0)

        chunks = [scalar_ref[i * 4 + k] for k in range(4)]
        low = jnp.concatenate([got_ref[c, :, 256:384] for c in chunks], axis=0)
        q_in = jnp.concatenate([q_ref[c] for c in chunks], axis=0).astype(F32)
        query = (
            q_in + SCALE * jnp.dot(low[:, 0:64], wq_ref[...], preferred_element_type=F32)
        ).astype(BF)
        query = jnp.concatenate([query[:, h * HEAD : (h + 1) * HEAD] for h in range(8)], axis=0)
        dout = dout_s[i]

        def place(t):
            return pl.multiple_of(PAD + high - KEY_CHUNK * (t + 1), BLOCK)

        m_s[...] = jnp.full_like(m_s, MASKED)

        def scores(t, masked):
            at = place(t)
            s = lax.dot_general(query, kv_s[pl.ds(at, KEY_CHUNK), 0:128], NT, preferred_element_type=F32)
            if masked:
                key = at - PAD + lax.broadcasted_iota(jnp.int32, (1, KEY_CHUNK), 1)
                s = jnp.where((key >= start) & (key <= row), s, MASKED)
            s_s[t] = s
            top = m_s[...]
            for c in range(KEY_CHUNK // 128):
                top = jnp.maximum(top, s[:, c * 128 : (c + 1) * 128])
            m_s[...] = top

        def clean_scores(t, _):
            scores(t, False)
            return 0

        def masked_scores(t, _):
            scores(t, True)
            return 0

        scores(0, True)
        lax.fori_loop(1, clean, clean_scores, 0)
        lax.fori_loop(clean, steps, masked_scores, 0)
        top = jnp.max(m_s[...], axis=1, keepdims=True)
        acc_s[...] = jnp.zeros_like(acc_s)

        def forward(t, _):
            w = jnp.exp2((s_s[t] - top) * (INVERSE * LOG2E)).astype(BF)
            w_s[t] = w
            acc_s[...] += jnp.dot(w, kv_s[pl.ds(place(t), KEY_CHUNK), 128:384], preferred_element_type=F32)
            return 0

        lax.fori_loop(0, steps, forward, 0)
        over = 1.0 / acc_s[:, 192:193]
        out = (acc_s[:, 0:128] * over).astype(BF)
        for h in range(8):
            out_ref[i, :, h * HEAD : (h + 1) * HEAD] = out[h * BLOCK : (h + 1) * BLOCK, :]
        wide = dout.astype(F32)
        delta = jnp.sum(wide * out.astype(F32), axis=1, keepdims=True) * over
        scaled = (wide * over).astype(BF)
        g = lax.dot_general(wv_ref[...], scaled, NT, preferred_element_type=F32).astype(BF)
        weighted_low = (acc_s[:, 128:256] * over).astype(BF)
        vup_s[...] += lax.dot_general(weighted_low, dout, TN, preferred_element_type=F32)
        dq_s[...] = jnp.zeros_like(dq_s)

        def backward(t, _):
            at = place(t)
            w = w_s[t]
            dp = lax.dot_general(scaled, kv_s[pl.ds(at, KEY_CHUNK), 128:256], NT, preferred_element_type=F32)
            ds = (w.astype(F32) * (dp - delta)).astype(BF)
            dq_s[...] += jnp.dot(ds, kv_s[pl.ds(at, KEY_CHUNK), 0:128], preferred_element_type=F32)
            t_s[:, pl.ds(at, KEY_CHUNK)] += jnp.dot(g, w, preferred_element_type=F32)
            return 0

        lax.fori_loop(0, steps, backward, 0)
        dq = (dq_s[...] * INVERSE).astype(BF)
        low_t = jnp.transpose(low.astype(F32))[0:64, :].astype(BF)
        lg = jnp.zeros((64, BLOCK), F32)
        for h in range(8):
            dq_h = dq[h * BLOCK : (h + 1) * BLOCK, :]
            lg = lg + lax.dot_general(
                wq_ref[:, h * HEAD : (h + 1) * HEAD], dq_h, NT, preferred_element_type=F32
            )
            qup_s[h] += jnp.dot(low_t, dq_h, preferred_element_type=F32)
        lg_s[i] = lg
        return 0

    lax.fori_loop(0, 4, turn_of, 0)

    for c in range(32):
        at = (scalar_ref[28] - c // 8 + 4) % 4
        own = jnp.where(scalar_ref[16 + at] == c, 1.0, 0.0)
        both = jnp.concatenate([lg_s[at] * own, t_s[:, PAD + c * BLOCK : PAD + (c + 1) * BLOCK]], axis=0)
        both = jnp.transpose(both) * SCALE
        source = kv_s[PAD + c * BLOCK : PAD + (c + 1) * BLOCK, 256:384].astype(F32)[:, 65:66]
        for g in range(4):
            chosen = jnp.where(source == g, both, 0.0)
            send_ref[g * 32 + c] = (
                chosen[0:32, :] + chosen[32:64, :] + chosen[64:96, :] + chosen[96:128, :]
            ).astype(BF)
    for c in range(2):
        for h in range(4):
            up_ref[c, h * 64 : (h + 1) * 64, :] = (qup_s[c * 4 + h] * SCALE).astype(BF)
        up_ref[c, 256:288, :] = (vup_s[c * 32 : (c + 1) * 32, :] * SCALE).astype(BF)


def attention(scalar, q, got, dout, notes, kv, wv, wq):
    chunks = 4096 // KEY_CHUNK
    return pl.pallas_call(
        attention_kernel,
        out_shape=(
            jax.ShapeDtypeStruct((4, BLOCK, 1024), BF),
            jax.ShapeDtypeStruct((128, QUARTER, 128), BF),
            jax.ShapeDtypeStruct((2, 288, 128), BF),
        ),
        in_specs=[scalars()]
        + [whole()] * 7
        + [pl.BlockSpec(memory_space=pl.ANY), whole(), whole()],
        out_specs=(whole(), whole(), whole()),
        scratch_shapes=[
            VMEM((PAD + 4096, 384), BF),
            VMEM((chunks, ROWS_STEP, KEY_CHUNK), F32),
            VMEM((chunks, ROWS_STEP, KEY_CHUNK), BF),
            VMEM((64, PAD + 4096), F32),
            VMEM((ROWS_STEP, 128), F32),
            VMEM((ROWS_STEP, 256), F32),
            VMEM((ROWS_STEP, 128), F32),
            VMEM((4, ROWS_STEP, 128), BF),
            VMEM((4, 64, BLOCK), F32),
            VMEM((8, 64, 128), F32),
            VMEM((128, 128), F32),
            pltpu.SMEM((4,), jnp.int32),
            pltpu.SemaphoreType.DMA((32,)),
        ],
        compiler_params=params(56),
        cost_estimate=pl.CostEstimate(flops=20 << 30, bytes_accessed=8 << 20, transcendentals=8 << 20),
    )(scalar, q, got, *dout, notes, kv, wv, wq)


def low_back_kernel(outgoing_ref, got_ref, low_ref, sum_ref):
    for r in range(4):
        total = got_ref[r * 32].astype(F32)
        for c in range(1, 32):
            total = total + got_ref[r * 32 + c].astype(F32)
        sum_ref[r] = total
    for k in range(4):
        low_ref[k * QUARTER : (k + 1) * QUARTER, :] = sum_ref[outgoing_ref[k]].astype(BF)


def low_back_of(outgoing, got):
    return pl.pallas_call(
        low_back_kernel,
        out_shape=jax.ShapeDtypeStruct((BLOCK, 128), BF),
        in_specs=[scalars(), whole()],
        out_specs=whole(),
        scratch_shapes=[VMEM((4, QUARTER, 128), F32)],
        cost_estimate=pl.CostEstimate(flops=1 << 19, bytes_accessed=1 << 20, transcendentals=0),
    )(outgoing, got)


def grad_kernel(place_ref, x_ref, other_ref, low_ref, low_other_ref, up_ref, up_other_ref, out_ref):
    j = pl.program_id(0)
    rows = jnp.concatenate([x_ref[...], other_ref[...]], axis=0)
    low = jnp.concatenate([low_ref[...], low_other_ref[...]], axis=0)
    grad = lax.dot_general(rows, low, TN, preferred_element_type=F32).astype(BF)
    for d in range(16):
        out_ref[d, 0:64, :] = grad[d * 64 : (d + 1) * 64, :]
    head = pl.ds(pl.multiple_of(j * 64, 64), 64)
    up = up_ref[0, head, :].astype(F32) + up_other_ref[head, :].astype(F32)
    tail = up_ref[0, 256:288, :].astype(F32) + up_other_ref[256:288, :].astype(F32)
    for y in range(4):
        keep = jnp.where(place_ref[1] == y, 1.0, 0.0)
        for x in range(4):
            out_ref[y * 4 + x, 64:80, :] = (up[x * 16 : (x + 1) * 16, :] * keep).astype(BF)
            low_rows = jnp.zeros((2, 128), F32)
            for dp in range(4):
                at = (dp * 4 + x) * 2
                low_rows = low_rows + tail[at : at + 2, :] * jnp.where(j == dp, keep, 0.0)
            out_ref[y * 4 + x, 80:SHARD, :] = jnp.concatenate(
                [low_rows, jnp.zeros((SHARD - 82, 128), F32)], axis=0
            ).astype(BF)


def grad_chunks(place, x, other, low, low_other, up, up_other):
    return pl.pallas_call(
        grad_kernel,
        out_shape=jax.ShapeDtypeStruct((64, SHARD, 128), BF),
        grid_spec=pltpu.PrefetchScalarGridSpec(
            num_scalar_prefetch=1,
            grid=(4,),
            in_specs=[
                pl.BlockSpec((BLOCK, 1024), lambda j, place: (0, place[0] * 4 + j)),
                pl.BlockSpec((BLOCK, 1024), lambda j, place: (0, j)),
                pl.BlockSpec((BLOCK, 128), lambda j, place: (0, 0)),
                pl.BlockSpec((BLOCK, 128), lambda j, place: (0, 0)),
                pl.BlockSpec((1, 288, 128), lambda j, place: (place[0], 0, 0)),
                pl.BlockSpec((288, 128), lambda j, place: (0, 0)),
            ],
            out_specs=pl.BlockSpec((16, SHARD, 128), lambda j, place: (j, 0, 0)),
        ),
        cost_estimate=pl.CostEstimate(flops=2 * 256 * 4096 * 128, bytes_accessed=4 << 20, transcendentals=0),
    )(place, x, other, low, low_other, up, up_other)


def gather_kernel(place_ref, own_ref, other_ref, down_ref, query_ref, value_ref):
    zero = place_ref[0] == 0
    for chip in range(64):
        dp, y, x = chip // 16, chip // 4 % 4, chip % 4
        own, other = own_ref[chip].astype(F32), other_ref[chip].astype(F32)
        for core in range(2):
            part = jnp.where(zero, own, other) if core == 0 else jnp.where(zero, other, own)
            down_ref[core * 4096 + chip * 64 : core * 4096 + (chip + 1) * 64, :] = part[0:64, :]
            column = (y * 8 + core * 4 + dp) * 128
            query_ref[x * 16 : (x + 1) * 16, column : column + 128] = part[64:80, :]
            row = core * 32 + (dp * 4 + x) * 2
            value_ref[row : row + 2, y * 128 : (y + 1) * 128] = part[80:82, :]


def gather_outputs(place, own, other):
    return pl.pallas_call(
        gather_kernel,
        out_shape=(
            jax.ShapeDtypeStruct((8192, 128), F32),
            jax.ShapeDtypeStruct((64, 4096), F32),
            jax.ShapeDtypeStruct((64, 512), F32),
        ),
        in_specs=[scalars(), whole(), whole()],
        out_specs=(whole(), whole(), whole()),
        compiler_params=params(32),
        cost_estimate=pl.CostEstimate(flops=1 << 20, bytes_accessed=8 << 20, transcendentals=0),
    )(place, own, other)


def join_kernel(place_ref, p0, p1, p2, p3, out_ref):
    for i, piece in enumerate((p0, p1, p2, p3)):
        column = (place_ref[1] + i) % 4 * 1024
        out_ref[0, :, pl.ds(pl.multiple_of(column, 1024), 1024)] = piece[...]


def join_heads(place, pieces):
    return pl.pallas_call(
        join_kernel,
        out_shape=jax.ShapeDtypeStruct((1, BLOCK, 4096), BF),
        in_specs=[scalars()] + [whole()] * 4,
        out_specs=whole(),
        cost_estimate=pl.CostEstimate(flops=0, bytes_accessed=2 << 20, transcendentals=0),
    )(place, *pieces)


def on_device(
    generated_input,
    frozen_query,
    frozen_key_value,
    adapter_down_weight,
    query_up_weight,
    value_up_weight,
    response_numbers,
    target_replica,
    output_gradient,
):
    me = lax.axis_index("dp")
    my_y = lax.axis_index("y")
    my_core = lax.axis_index("core")
    my_lane = lax.axis_index("x") * 2 + my_core
    places = jnp.arange(4, dtype=jnp.int32)
    route = target_replica[0]
    outgoing = lax.dynamic_index_in_dim(route, me, 0, keepdims=False)
    send_order = jnp.sum(places[None, :] * (outgoing[None, :] == places[:, None]), axis=1).astype(jnp.int32)
    place = jnp.stack([my_core, my_y]).astype(jnp.int32)
    swap = [(0, 1), (1, 0)]

    rows = generated_input[0]
    sent = front(send_order, rows, adapter_down_weight, frozen_key_value[0])

    row = (my_y - places + 4) % 4
    notes = jnp.concatenate([response_numbers[0], route.reshape(16), jnp.zeros((112,), jnp.int32)])
    notes, sent = lax.optimization_barrier((notes.reshape(2, 128), sent))
    notes = jnp.stack([notes] + [lax.ppermute(notes, "y", turn(d)) for d in range(1, 4)])
    resp = notes[:, 0, :]
    routes = notes[:, 1, 0:16].reshape(4, 4, 4)
    mine = (routes == me).astype(jnp.int32)
    order = (jnp.sum(mine * places[None, :, None], axis=1) * 4 + row[:, None]).reshape(16)
    block = row * 8 + my_lane
    scalar = jnp.concatenate([order, block, resp[:, 0], resp[:, 127], row]).astype(jnp.int32)

    got = lax.all_to_all(sent, ROWS, 0, 0, tiled=True)
    gradient = output_gradient[0]
    dout = []
    for d in range(4):
        part = lax.dynamic_slice_in_dim(gradient, (my_y + d) % 4 * 1024, 1024, 1)
        dout.append(lax.ppermute(part, "y", turn(d)) if d else part)
    wv = lax.dynamic_slice_in_dim(value_up_weight, my_y * 128, 128, 1)
    wq = lax.dynamic_slice_in_dim(query_up_weight, my_y * 1024, 1024, 1)
    packed = pack(scalar, got, notes, wv)
    kv = lax.all_gather(packed, ("x", "core"), axis=0, tiled=False)
    q = lax.all_to_all(
        query_chunks(send_order, frozen_query[0]), ROWS, 0, 0, tiled=True
    )
    other_half = lax.ppermute(
        lax.dynamic_slice_in_dim(rows, (1 - my_core) * 4096, 4096, 1), "core", swap
    )

    out, send, up = attention(scalar, q, got, dout, notes, kv, wv, wq)
    pieces = [out[0]] + [lax.ppermute(out[i], "y", turn(-i)) for i in range(1, 4)]
    up_other = lax.ppermute(
        lax.dynamic_index_in_dim(up, 1 - my_core, 0, keepdims=False), "core", swap
    )
    low_back = low_back_of(outgoing, lax.all_to_all(send, ALL, 0, 0, tiled=True))
    low_back, pieces = lax.optimization_barrier((low_back, pieces))
    low_other = lax.ppermute(low_back, "core", swap)
    chunks = grad_chunks(place, rows, other_half, low_back, low_other, up, up_other)
    parts = lax.all_to_all(chunks, CHIP, 0, 0, tiled=True)
    shard = jnp.sum(parts.astype(F32), axis=0).astype(BF)
    own = lax.all_to_all(jnp.broadcast_to(shard[None], parts.shape), CHIP, 0, 0, tiled=True)
    other = lax.ppermute(own, "core", swap)
    grad_a, query_up_gradient, value_up_gradient = gather_outputs(place, own, other)

    attn_out = join_heads(place, pieces)
    return (attn_out, grad_a, query_up_gradient, value_up_gradient)


def solution(mesh):
    grid = Mesh(mesh.devices.reshape(4, 4, 4, 2), ("dp", "y", "x", "core"))
    ctx = ("y", "x", "core")
    return jax.shard_map(
        on_device,
        mesh=grid,
        in_specs=(
            P("dp", ctx, None),
            P("dp", ctx, None),
            P("dp", ctx, None),
            P(),
            P(),
            P(),
            P("dp", ctx),
            P(ctx, None, None),
            P("dp", ctx, None),
        ),
        out_specs=(P("dp", ctx, None), P(), P(), P()),
        check_vma=False,
    )
```

```python
import functools
import math

import jax
import jax.numpy as jnp
from jax import lax
from jax.experimental import pallas as pl
from jax.experimental.pallas import tpu as pltpu
from jax.sharding import Mesh
from jax.sharding import PartitionSpec as P

HEAD = 128
BLOCK = 128
QUARTER = 32
KEY_CHUNK = 512
HALF = KEY_CHUNK // 2
PAD = KEY_CHUNK - BLOCK
ROWS_STEP = 8 * BLOCK
SCALE = 0.5
MASKED = -1e30
INVERSE = 1.0 / math.sqrt(HEAD)
LOG2E = 1.4426950408889634
BF = jnp.bfloat16
F32 = jnp.float32
NT = (((1,), (1,)), ((), ()))
TN = (((0,), (0,)), ((), ()))
VMEM = pltpu.VMEM
CHIP = ("dp", "y", "x")
ROWS = ("dp", "y")
SHARD = 88


def turn(d):
    return [(y, (y + d) % 4) for y in range(4)]


def whole():
    return pl.BlockSpec(memory_space=pltpu.VMEM)


def scalars():
    return pl.BlockSpec(memory_space=pltpu.SMEM)


def params(mib):
    return pltpu.CompilerParams(vmem_limit_bytes=mib << 20)


def quarter_rows(route_ref, r):
    me = lax.axis_index("dp")
    quarter = sum(jnp.where(route_ref[0, me, k] == r, k, 0) for k in range(1, 4))
    return pl.ds(pl.multiple_of(quarter * QUARTER, QUARTER), QUARTER)


def front_kernel(route_ref, x_ref, a_ref, kv_ref, resp_ref, out_ref, note_ref, acc_ref, low_ref):
    step = pl.program_id(0)

    @pl.when(step == 0)
    def _():
        acc_ref[...] = jnp.zeros_like(acc_ref)

    acc_ref[...] += jnp.dot(x_ref[...], a_ref[...], preferred_element_type=F32)

    @pl.when(step == pl.num_programs(0) - 1)
    def _():
        lane = lax.broadcasted_iota(jnp.int32, (1, 128), 1)
        note = jnp.zeros((1, 128), jnp.int32)
        for g in range(4):
            for k in range(4):
                note = jnp.where(lane == g * 4 + k, route_ref[0, g, k], note)
        note_ref[0:1, :] = resp_ref[...]
        note_ref[1:2, :] = note
        low_ref[...] = acc_ref[...].astype(BF)
        for r in range(4):
            rows = quarter_rows(route_ref, r)
            low = low_ref[rows, :]
            for y in range(4):
                out_ref[r * 4 + y, :, 0:128] = kv_ref[rows, y * 128 : y * 128 + 128]
                out_ref[r * 4 + y, :, 128:256] = kv_ref[rows, 512 + y * 128 : 640 + y * 128]
                out_ref[r * 4 + y, :, 256:384] = low


def front(route, x, a, kv, resp):
    steps = 2
    part = 8192 // steps
    return pl.pallas_call(
        front_kernel,
        out_shape=(
            jax.ShapeDtypeStruct((16, QUARTER, 384), BF),
            jax.ShapeDtypeStruct((2, 128), jnp.int32),
        ),
        grid=(steps,),
        in_specs=[
            scalars(),
            pl.BlockSpec((BLOCK, part), lambda i: (0, i)),
            pl.BlockSpec((part, 128), lambda i: (i, 0)),
            pl.BlockSpec((BLOCK, 1024), lambda i: (0, 0)),
            pl.BlockSpec((1, BLOCK), lambda i: (0, 0)),
        ],
        out_specs=(
            pl.BlockSpec((16, QUARTER, 384), lambda i: (0, 0, 0)),
            pl.BlockSpec((2, 128), lambda i: (0, 0)),
        ),
        scratch_shapes=[VMEM((BLOCK, 128), F32), VMEM((BLOCK, 128), BF)],
        compiler_params=params(58),
        cost_estimate=pl.CostEstimate(flops=2 * 128 * 8192 * 128, bytes_accessed=5 << 20, transcendentals=0),
    )(route, x, a, kv, resp)


def query_chunks_kernel(route_ref, q_ref, out_ref, sem):
    copies = []
    for r in range(4):
        rows = quarter_rows(route_ref, r)
        for y in range(4):
            copies.append(
                pltpu.make_async_copy(
                    q_ref.at[rows, pl.ds(y * 1024, 1024)], out_ref.at[r * 4 + y], sem.at[r * 4 + y]
                )
            )
    for copy in copies:
        copy.start()
    for copy in copies:
        copy.wait()


def query_chunks(route, q):
    return pl.pallas_call(
        query_chunks_kernel,
        out_shape=jax.ShapeDtypeStruct((16, QUARTER, 1024), BF),
        in_specs=[scalars(), pl.BlockSpec(memory_space=pl.ANY)],
        out_specs=pl.BlockSpec(memory_space=pl.ANY),
        scratch_shapes=[pltpu.SemaphoreType.DMA((16,))],
        compiler_params=params(48),
        cost_estimate=pl.CostEstimate(flops=0, bytes_accessed=2 << 20, transcendentals=0),
    )(route, q)


def pack_kernel(scalar_ref, got_ref, notes_ref, wv_ref, out_ref):
    lane = lax.broadcasted_iota(jnp.int32, (1, 64), 1)
    for i in range(4):
        y = scalar_ref[28 + i]
        extra = jnp.where(lane == 0, 1.0, 0.0)
        for k in range(4):
            source = (scalar_ref[i * 4 + k] // 4).astype(F32)
            extra = jnp.where(lane == 1 + k, source, extra)
        for v in range(1, 4):
            below = jnp.sum(jnp.where(notes_ref[i, 0:1, :] < v, 1.0, 0.0), axis=1, keepdims=True)
            extra = jnp.where(lane == 4 + v, below, extra)
        rows = jnp.concatenate([got_ref[scalar_ref[i * 4 + k]] for k in range(4)], axis=0)
        low_v = rows[:, 320:384]
        value = rows[:, 128:256].astype(F32) + SCALE * jnp.dot(
            low_v, wv_ref[...], preferred_element_type=F32
        )
        extra = jnp.broadcast_to(extra, (BLOCK, 64))
        out_ref[y, :, 0:128] = rows[:, 0:128]
        out_ref[y, :, 128:256] = value.astype(BF)
        out_ref[y, :, 256:384] = jnp.concatenate([low_v.astype(F32), extra], axis=1).astype(BF)


def pack(scalar, got, notes, wv):
    return pl.pallas_call(
        pack_kernel,
        out_shape=jax.ShapeDtypeStruct((4, BLOCK, 384), BF),
        in_specs=[scalars(), whole(), whole(), whole()],
        out_specs=whole(),
        cost_estimate=pl.CostEstimate(flops=1 << 23, bytes_accessed=1 << 20, transcendentals=0),
    )(scalar, got, notes, wv)


def attention_kernel(
    scalar_ref, q_ref, got_ref, d0, d1, d2, d3, notes_ref, kv_ref, wv_ref, wq_ref,
    out_ref, send_ref, send_other_ref, up_ref, up_other_ref,
    kv_s, s_s, w_s, t_s, m_s, acc_s, dq_s, dout_s, lg_s, qup_s, vup_s, send_s, up_s, below_s, sem,
):
    copies = []
    for c in range(32):
        copies.append(
            pltpu.make_async_copy(
                kv_ref.at[c % 8, c // 8], kv_s.at[pl.ds(PAD + c * BLOCK, BLOCK), :], sem.at[c]
            )
        )
    for copy in copies:
        copy.start()
    kv_s[0:PAD, :] = jnp.zeros((PAD, 384), BF)
    t_s[...] = jnp.zeros_like(t_s)
    qup_s[...] = jnp.zeros_like(qup_s)
    vup_s[...] = jnp.zeros_like(vup_s)
    for i, d in enumerate((d0, d1, d2, d3)):
        for h in range(8):
            dout_s[i, h * BLOCK : (h + 1) * BLOCK, :] = d[:, h * HEAD : (h + 1) * HEAD]
    for copy in copies:
        copy.wait()
    counts = kv_s[PAD : PAD + 16, 256:384].astype(F32)
    for c in range(1, 32):
        counts = counts + kv_s[PAD + c * BLOCK : PAD + c * BLOCK + 16, 256:384].astype(F32)
    lane = lax.broadcasted_iota(jnp.int32, (1, 128), 1)
    below_s[0] = 0
    for v in range(1, 4):
        below_s[v] = jnp.sum(jnp.where(lane == 68 + v, counts[0:1, :], 0.0)).astype(jnp.int32)
    diagonal = lax.broadcasted_iota(jnp.int32, (BLOCK, BLOCK), 0) == lax.broadcasted_iota(
        jnp.int32, (BLOCK, BLOCK), 1
    )

    def turn_of(i, _):
        block = scalar_ref[16 + i]
        high = (block + 1) * BLOCK
        width = high - below_s[scalar_ref[20 + i]]
        steps = (width + HALF - 1) // KEY_CHUNK
        half = width > steps * KEY_CHUNK
        clean = jnp.maximum(jnp.minimum((high - below_s[scalar_ref[24 + i]]) // KEY_CHUNK, steps), 1)
        resp = notes_ref[i, 0:1, :]
        start = jnp.zeros((1, BLOCK), jnp.int32)
        for v in range(1, 4):
            start = jnp.where(resp == v, below_s[v], start)
        start = jnp.sum(jnp.where(diagonal, start.astype(F32), 0.0), axis=1, keepdims=True).astype(jnp.int32)
        start = jnp.concatenate([start] * 8, axis=0)
        row = block * BLOCK + lax.broadcasted_iota(jnp.int32, (BLOCK, 1), 0)
        row = jnp.concatenate([row] * 8, axis=0)

        chunks = [scalar_ref[i * 4 + k] for k in range(4)]
        low = jnp.concatenate([got_ref[c, :, 256:384] for c in chunks], axis=0)
        q_in = jnp.concatenate([q_ref[c] for c in chunks], axis=0).astype(F32)
        query = (
            q_in + SCALE * jnp.dot(low[:, 0:64], wq_ref[...], preferred_element_type=F32)
        ).astype(BF)
        query = jnp.concatenate([query[:, h * HEAD : (h + 1) * HEAD] for h in range(8)], axis=0)
        dout = dout_s[i]

        def place(t, size):
            return pl.multiple_of(PAD + high - KEY_CHUNK * t - size, BLOCK)

        m_s[...] = jnp.full_like(m_s, MASKED)

        def scores(t, size, masked):
            at = place(t, size)
            s = lax.dot_general(query, kv_s[pl.ds(at, size), 0:128], NT, preferred_element_type=F32)
            if masked:
                key = at - PAD + lax.broadcasted_iota(jnp.int32, (1, size), 1)
                s = jnp.where((key >= start) & (key <= row), s, MASKED)
            s_s[t, :, 0:size] = s
            top = m_s[...]
            for c in range(size // 128):
                top = jnp.maximum(top, s[:, c * 128 : (c + 1) * 128])
            m_s[...] = top

        def clean_scores(t, _):
            scores(t, KEY_CHUNK, False)
            return 0

        def masked_scores(t, _):
            scores(t, KEY_CHUNK, True)
            return 0

        lax.fori_loop(0, jnp.minimum(steps, 1), masked_scores, 0)
        lax.fori_loop(1, clean, clean_scores, 0)
        lax.fori_loop(clean, steps, masked_scores, 0)

        @pl.when(half)
        def _():
            scores(steps, HALF, True)

        top = jnp.max(m_s[...], axis=1, keepdims=True)
        acc_s[...] = jnp.zeros_like(acc_s)

        def forward(t, size):
            w = jnp.exp2((s_s[t, :, 0:size] - top) * (INVERSE * LOG2E)).astype(BF)
            w_s[t, :, 0:size] = w
            acc_s[...] += jnp.dot(w, kv_s[pl.ds(place(t, size), size), 128:384], preferred_element_type=F32)

        def forward_step(t, _):
            forward(t, KEY_CHUNK)
            return 0

        lax.fori_loop(0, steps, forward_step, 0)

        @pl.when(half)
        def _():
            forward(steps, HALF)

        over = 1.0 / acc_s[:, 192:193]
        out = (acc_s[:, 0:128] * over).astype(BF)
        for h in range(8):
            out_ref[i, :, h * HEAD : (h + 1) * HEAD] = out[h * BLOCK : (h + 1) * BLOCK, :]
        wide = dout.astype(F32)
        delta = jnp.sum(wide * out.astype(F32), axis=1, keepdims=True) * over
        scaled = (wide * over).astype(BF)
        g = lax.dot_general(wv_ref[...], scaled, NT, preferred_element_type=F32).astype(BF)
        weighted_low = (acc_s[:, 128:256] * over).astype(BF)
        vup_s[...] += lax.dot_general(weighted_low, dout, TN, preferred_element_type=F32)
        dq_s[...] = jnp.zeros_like(dq_s)

        def backward(t, size):
            at = place(t, size)
            w = w_s[t, :, 0:size]
            dp = lax.dot_general(scaled, kv_s[pl.ds(at, size), 128:256], NT, preferred_element_type=F32)
            ds = (w.astype(F32) * (dp - delta)).astype(BF)
            dq_s[...] += jnp.dot(ds, kv_s[pl.ds(at, size), 0:128], preferred_element_type=F32)
            t_s[:, pl.ds(at, size)] += jnp.dot(g, w, preferred_element_type=F32)

        def backward_step(t, _):
            backward(t, KEY_CHUNK)
            return 0

        lax.fori_loop(0, steps, backward_step, 0)

        @pl.when(half)
        def _():
            backward(steps, HALF)

        dq = (dq_s[...] * INVERSE).astype(BF)
        low_t = jnp.transpose(low.astype(F32))[0:64, :].astype(BF)
        lg = jnp.zeros((64, BLOCK), F32)
        for h in range(8):
            dq_h = dq[h * BLOCK : (h + 1) * BLOCK, :]
            lg = lg + lax.dot_general(
                wq_ref[:, h * HEAD : (h + 1) * HEAD], dq_h, NT, preferred_element_type=F32
            )
            qup_s[h] += jnp.dot(low_t, dq_h, preferred_element_type=F32)
        lg_s[i] = lg
        return 0

    lax.fori_loop(0, 4, turn_of, 0)

    token_row = lax.broadcasted_iota(jnp.int32, (1, BLOCK), 1)
    token = lax.broadcasted_iota(jnp.int32, (BLOCK, BLOCK), 1)
    slot = lax.broadcasted_iota(jnp.int32, (BLOCK, BLOCK), 0)
    within = token % QUARTER == slot % QUARTER
    wanted = (slot // QUARTER).astype(F32)
    for c in range(32):
        at = (scalar_ref[28] - c // 8 + 4) % 4
        own = jnp.where(scalar_ref[16 + at] == c, 1.0, 0.0)
        both = jnp.concatenate([lg_s[at] * own, t_s[:, PAD + c * BLOCK : PAD + (c + 1) * BLOCK]], axis=0)
        both = (both * SCALE).astype(BF)
        note = kv_s[PAD + c * BLOCK : PAD + c * BLOCK + 16, 256:384].astype(F32)[0:1, :]
        source = note[:, 65:66]
        for k in range(1, 4):
            source = jnp.where(token_row // QUARTER == k, note[:, 65 + k : 66 + k], source)
        pick = jnp.where(within & (source == wanted), 1.0, 0.0).astype(BF)
        sent = lax.dot_general(pick, both, NT, preferred_element_type=F32).astype(BF)
        for g in range(4):
            send_s[c % 2, g * 16 + c // 2] = sent[g * QUARTER : (g + 1) * QUARTER, :]
    for c in range(2):
        for h in range(4):
            up_s[c, h * 64 : (h + 1) * 64, :] = (qup_s[c * 4 + h] * SCALE).astype(BF)
        up_s[c, 256:288, :] = (vup_s[c * 32 : (c + 1) * 32, :] * SCALE).astype(BF)
    core = lax.axis_index("core")
    send_ref[...] = send_s[core]
    send_other_ref[...] = send_s[1 - core]
    up_ref[...] = up_s[core]
    up_other_ref[...] = up_s[1 - core]


def attention(scalar, q, got, dout, notes, kv, wv, wq):
    chunks = 4096 // KEY_CHUNK
    return pl.pallas_call(
        attention_kernel,
        out_shape=(
            jax.ShapeDtypeStruct((4, BLOCK, 1024), BF),
            jax.ShapeDtypeStruct((64, QUARTER, 128), BF),
            jax.ShapeDtypeStruct((64, QUARTER, 128), BF),
            jax.ShapeDtypeStruct((288, 128), BF),
            jax.ShapeDtypeStruct((288, 128), BF),
        ),
        in_specs=[scalars()]
        + [whole()] * 7
        + [pl.BlockSpec(memory_space=pl.ANY), whole(), whole()],
        out_specs=(whole(),) * 5,
        scratch_shapes=[
            VMEM((PAD + 4096, 384), BF),
            VMEM((chunks, ROWS_STEP, KEY_CHUNK), F32),
            VMEM((chunks, ROWS_STEP, KEY_CHUNK), BF),
            VMEM((64, PAD + 4096), F32),
            VMEM((ROWS_STEP, 128), F32),
            VMEM((ROWS_STEP, 256), F32),
            VMEM((ROWS_STEP, 128), F32),
            VMEM((4, ROWS_STEP, 128), BF),
            VMEM((4, 64, BLOCK), F32),
            VMEM((8, 64, 128), F32),
            VMEM((128, 128), F32),
            VMEM((2, 64, QUARTER, 128), BF),
            VMEM((2, 288, 128), BF),
            pltpu.SMEM((4,), jnp.int32),
            pltpu.SemaphoreType.DMA((32,)),
        ],
        compiler_params=params(56),
        cost_estimate=pl.CostEstimate(flops=20 << 30, bytes_accessed=8 << 20, transcendentals=8 << 20),
    )(scalar, q, got, *dout, notes, kv, wv, wq)


def low_back_kernel(route_ref, got_ref, low_ref, sum_ref):
    me = lax.axis_index("dp")
    for r in range(4):
        total = got_ref[r * 16].astype(F32)
        for c in range(1, 16):
            total = total + got_ref[r * 16 + c].astype(F32)
        sum_ref[r] = total
    for k in range(4):
        low_ref[k * QUARTER : (k + 1) * QUARTER, :] = sum_ref[route_ref[0, me, k]].astype(BF)


def low_back_of(route, got):
    return pl.pallas_call(
        low_back_kernel,
        out_shape=jax.ShapeDtypeStruct((BLOCK, 128), BF),
        in_specs=[scalars(), whole()],
        out_specs=whole(),
        scratch_shapes=[VMEM((4, QUARTER, 128), F32)],
        cost_estimate=pl.CostEstimate(flops=1 << 19, bytes_accessed=1 << 20, transcendentals=0),
    )(route, got)


def grad_kernel(x_ref, other_ref, low_ref, low_other_ref, up_ref, up_other_ref, out_ref, own_s, sem):
    half = pl.ds(pl.multiple_of(lax.axis_index("core") * 4096, 4096), 4096)
    copy = pltpu.make_async_copy(x_ref.at[:, half], own_s, sem)
    copy.start()
    my_y = lax.axis_index("y")
    low = jnp.concatenate([low_ref[...], low_other_ref[...]], axis=0)
    up = up_ref[...].astype(F32) + up_other_ref[...].astype(F32)
    for d in range(64):
        dp, y, x = d // 16, d // 4 % 4, d % 4
        keep = jnp.where(my_y == y, 1.0, 0.0)
        first = 256 + (dp * 4 + x) * 2
        tail = jnp.concatenate([up[first : first + 2, :] * keep, jnp.zeros((SHARD - 82, 128), F32)], axis=0)
        out_ref[d, 64:80, :] = (up[dp * 64 + x * 16 : dp * 64 + (x + 1) * 16, :] * keep).astype(BF)
        out_ref[d, 80:SHARD, :] = tail.astype(BF)
    copy.wait()
    for j in range(4):
        span = slice(j * 1024, (j + 1) * 1024)
        rows = jnp.concatenate([own_s[:, span], other_ref[:, span]], axis=0)
        grad = lax.dot_general(rows, low, TN, preferred_element_type=F32).astype(BF)
        for d in range(16):
            out_ref[j * 16 + d, 0:64, :] = grad[d * 64 : (d + 1) * 64, :]


def grad_chunks(x, other, low, low_other, up, up_other):
    return pl.pallas_call(
        grad_kernel,
        out_shape=jax.ShapeDtypeStruct((64, SHARD, 128), BF),
        in_specs=[pl.BlockSpec(memory_space=pl.ANY)] + [whole()] * 5,
        out_specs=whole(),
        scratch_shapes=[VMEM((BLOCK, 4096), BF), pltpu.SemaphoreType.DMA],
        compiler_params=params(48),
        cost_estimate=pl.CostEstimate(flops=2 * 256 * 4096 * 128, bytes_accessed=4 << 20, transcendentals=0),
    )(x, other, low, low_other, up, up_other)


def gather_kernel(own_ref, other_ref, down_ref, query_ref, value_ref):
    zero = lax.axis_index("core") == 0
    for chip in range(64):
        dp, y, x = chip // 16, chip // 4 % 4, chip % 4
        own, other = own_ref[chip].astype(F32), other_ref[chip].astype(F32)
        for core in range(2):
            part = jnp.where(zero, own, other) if core == 0 else jnp.where(zero, other, own)
            down_ref[core * 4096 + chip * 64 : core * 4096 + (chip + 1) * 64, :] = part[0:64, :]
            column = (y * 8 + core * 4 + dp) * 128
            query_ref[x * 16 : (x + 1) * 16, column : column + 128] = part[64:80, :]
            row = core * 32 + (dp * 4 + x) * 2
            value_ref[row : row + 2, y * 128 : (y + 1) * 128] = part[80:82, :]


def gather_outputs(own, other):
    return pl.pallas_call(
        gather_kernel,
        out_shape=(
            jax.ShapeDtypeStruct((8192, 128), F32),
            jax.ShapeDtypeStruct((64, 4096), F32),
            jax.ShapeDtypeStruct((64, 512), F32),
        ),
        in_specs=[whole(), whole()],
        out_specs=(whole(), whole(), whole()),
        compiler_params=params(32),
        cost_estimate=pl.CostEstimate(flops=1 << 20, bytes_accessed=8 << 20, transcendentals=0),
    )(own, other)


def join_kernel(p0, p1, p2, p3, out_ref):
    for i, piece in enumerate((p0, p1, p2, p3)):
        column = (lax.axis_index("y") + i) % 4 * 1024
        out_ref[0, :, pl.ds(pl.multiple_of(column, 1024), 1024)] = piece[...]


def join_heads(pieces):
    return pl.pallas_call(
        join_kernel,
        out_shape=jax.ShapeDtypeStruct((1, BLOCK, 4096), BF),
        in_specs=[whole()] * 4,
        out_specs=whole(),
        cost_estimate=pl.CostEstimate(flops=0, bytes_accessed=2 << 20, transcendentals=0),
    )(*pieces)


def on_device(
    generated_input,
    frozen_query,
    frozen_key_value,
    adapter_down_weight,
    query_up_weight,
    value_up_weight,
    response_numbers,
    target_replica,
    output_gradient,
):
    me = lax.axis_index("dp")
    my_y = lax.axis_index("y")
    my_core = lax.axis_index("core")
    my_lane = lax.axis_index("x") * 2 + my_core
    places = jnp.arange(4, dtype=jnp.int32)
    swap = [(0, 1), (1, 0)]

    rows = generated_input[0]
    sent, notes = front(target_replica, rows, adapter_down_weight, frozen_key_value[0], response_numbers)

    row = (my_y - places + 4) % 4
    notes = jnp.stack([notes] + [lax.ppermute(notes, "y", turn(d)) for d in range(1, 4)])
    resp = notes[:, 0, :]
    routes = notes[:, 1, 0:16].reshape(4, 4, 4)
    mine = (routes == me).astype(jnp.int32)
    order = (jnp.sum(mine * places[None, :, None], axis=1) * 4 + row[:, None]).reshape(16)
    block = row * 8 + my_lane
    scalar = jnp.concatenate([order, block, resp[:, 0], resp[:, 127], row]).astype(jnp.int32)

    got = lax.all_to_all(sent, ROWS, 0, 0, tiled=True)
    gradient = output_gradient[0]
    dout = []
    for d in range(4):
        part = lax.dynamic_slice_in_dim(gradient, (my_y + d) % 4 * 1024, 1024, 1)
        dout.append(lax.ppermute(part, "y", turn(d)) if d else part)
    wv = lax.dynamic_slice_in_dim(value_up_weight, my_y * 128, 128, 1)
    wq = lax.dynamic_slice_in_dim(query_up_weight, my_y * 1024, 1024, 1)
    packed = pack(scalar, got, notes, wv)
    kv = lax.all_gather(packed, ("x", "core"), axis=0, tiled=False)
    q = lax.all_to_all(
        query_chunks(target_replica, frozen_query[0]), ROWS, 0, 0, tiled=True
    )
    other_half = lax.ppermute(
        lax.dynamic_slice_in_dim(rows, (1 - my_core) * 4096, 4096, 1), "core", swap
    )

    out, send, send_other, up, up_other = attention(scalar, q, got, dout, notes, kv, wv, wq)
    pieces = [out[0]] + [lax.ppermute(out[i], "y", turn(-i)) for i in range(1, 4)]
    up_other = lax.ppermute(up_other, "core", swap)
    send_other = lax.ppermute(send_other, "core", swap)
    send = (send.astype(F32) + send_other.astype(F32)).astype(BF)
    low_back = low_back_of(target_replica, lax.all_to_all(send, CHIP, 0, 0, tiled=True))
    low_other = lax.ppermute(low_back, "core", swap)
    chunks = grad_chunks(rows, other_half, low_back, low_other, up, up_other)
    parts = lax.all_to_all(chunks, CHIP, 0, 0, tiled=True)
    shard = jnp.sum(parts.astype(F32), axis=0).astype(BF)
    shard, pieces[2] = lax.optimization_barrier((shard, pieces[2]))
    own = lax.all_to_all(jnp.broadcast_to(shard[None], parts.shape), CHIP, 0, 0, tiled=True)
    own, pieces[1], pieces[3] = lax.optimization_barrier((own, pieces[1], pieces[3]))
    other = lax.ppermute(own, "core", swap)
    attn_out = join_heads(pieces)
    grad_a, query_up_gradient, value_up_gradient = gather_outputs(own, other)

    return (attn_out, grad_a, query_up_gradient, value_up_gradient)


def solution(mesh):
    grid = Mesh(mesh.devices.reshape(4, 4, 4, 2), ("dp", "y", "x", "core"))
    ctx = ("y", "x", "core")
    return jax.shard_map(
        on_device,
        mesh=grid,
        in_specs=(
            P("dp", ctx, None),
            P("dp", ctx, None),
            P("dp", ctx, None),
            P(),
            P(),
            P(),
            P("dp", ctx),
            P(ctx, None, None),
            P("dp", ctx, None),
        ),
        out_specs=(P("dp", ctx, None), P(), P(), P()),
        check_vma=False,
    )
```

```python
import functools
import math

import jax
import jax.numpy as jnp
from jax import lax
from jax.experimental import pallas as pl
from jax.experimental.pallas import tpu as pltpu
from jax.sharding import Mesh
from jax.sharding import PartitionSpec as P

HEAD = 128
BLOCK = 128
QUARTER = 32
KEY_CHUNK = 512
HALF = KEY_CHUNK // 2
PAD = KEY_CHUNK - BLOCK
ROWS_STEP = 8 * BLOCK
SCALE = 0.5
MASKED = -1e30
INVERSE = 1.0 / math.sqrt(HEAD)
LOG2E = 1.4426950408889634
BF = jnp.bfloat16
F32 = jnp.float32
NT = (((1,), (1,)), ((), ()))
TN = (((0,), (0,)), ((), ()))
VMEM = pltpu.VMEM
CHIP = ("dp", "y", "x")
ROWS = ("dp", "y")


def turn(d):
    return [(y, (y + d) % 4) for y in range(4)]


def whole():
    return pl.BlockSpec(memory_space=pltpu.VMEM)


def scalars():
    return pl.BlockSpec(memory_space=pltpu.SMEM)


def params(mib):
    return pltpu.CompilerParams(vmem_limit_bytes=mib << 20)


def quarter_rows(route_ref, r):
    me = lax.axis_index("dp")
    quarter = sum(jnp.where(route_ref[0, me, k] == r, k, 0) for k in range(1, 4))
    return pl.ds(pl.multiple_of(quarter * QUARTER, QUARTER), QUARTER)


def front_kernel(route_ref, x_ref, a_ref, kv_ref, resp_ref, out_ref, note_ref, acc_ref, low_ref):
    step = pl.program_id(0)

    @pl.when(step == 0)
    def _():
        acc_ref[...] = jnp.zeros_like(acc_ref)

    acc_ref[...] += jnp.dot(x_ref[...], a_ref[...], preferred_element_type=F32)

    @pl.when(step == pl.num_programs(0) - 1)
    def _():
        lane = lax.broadcasted_iota(jnp.int32, (1, 128), 1)
        note = jnp.zeros((1, 128), jnp.int32)
        for g in range(4):
            for k in range(4):
                note = jnp.where(lane == g * 4 + k, route_ref[0, g, k], note)
        note_ref[0:1, :] = resp_ref[...]
        note_ref[1:2, :] = note
        low_ref[...] = acc_ref[...].astype(BF)
        for r in range(4):
            rows = quarter_rows(route_ref, r)
            low = low_ref[rows, :]
            for y in range(4):
                out_ref[r * 4 + y, :, 0:128] = kv_ref[rows, y * 128 : y * 128 + 128]
                out_ref[r * 4 + y, :, 128:256] = kv_ref[rows, 512 + y * 128 : 640 + y * 128]
                out_ref[r * 4 + y, :, 256:384] = low


def front(route, x, a, kv, resp):
    steps = 2
    part = 8192 // steps
    return pl.pallas_call(
        front_kernel,
        out_shape=(
            jax.ShapeDtypeStruct((16, QUARTER, 384), BF),
            jax.ShapeDtypeStruct((2, 128), jnp.int32),
        ),
        grid=(steps,),
        in_specs=[
            scalars(),
            pl.BlockSpec((BLOCK, part), lambda i: (0, i)),
            pl.BlockSpec((part, 128), lambda i: (i, 0)),
            pl.BlockSpec((BLOCK, 1024), lambda i: (0, 0)),
            pl.BlockSpec((1, BLOCK), lambda i: (0, 0)),
        ],
        out_specs=(
            pl.BlockSpec((16, QUARTER, 384), lambda i: (0, 0, 0)),
            pl.BlockSpec((2, 128), lambda i: (0, 0)),
        ),
        scratch_shapes=[VMEM((BLOCK, 128), F32), VMEM((BLOCK, 128), BF)],
        compiler_params=params(58),
        cost_estimate=pl.CostEstimate(flops=2 * 128 * 8192 * 128, bytes_accessed=5 << 20, transcendentals=0),
    )(route, x, a, kv, resp)


def query_chunks_kernel(route_ref, q_ref, out_ref, sem):
    copies = []
    for r in range(4):
        rows = quarter_rows(route_ref, r)
        for y in range(4):
            copies.append(
                pltpu.make_async_copy(
                    q_ref.at[rows, pl.ds(y * 1024, 1024)], out_ref.at[r * 4 + y], sem.at[r * 4 + y]
                )
            )
    for copy in copies:
        copy.start()
    for copy in copies:
        copy.wait()


def query_chunks(route, q):
    return pl.pallas_call(
        query_chunks_kernel,
        out_shape=jax.ShapeDtypeStruct((16, QUARTER, 1024), BF),
        in_specs=[scalars(), pl.BlockSpec(memory_space=pl.ANY)],
        out_specs=pl.BlockSpec(memory_space=pl.ANY),
        scratch_shapes=[pltpu.SemaphoreType.DMA((16,))],
        compiler_params=params(48),
        cost_estimate=pl.CostEstimate(flops=0, bytes_accessed=2 << 20, transcendentals=0),
    )(route, q)


def pack_kernel(scalar_ref, got_ref, notes_ref, wv_ref, out_ref):
    lane = lax.broadcasted_iota(jnp.int32, (1, 64), 1)
    for i in range(4):
        y = scalar_ref[28 + i]
        extra = jnp.where(lane == 0, 1.0, 0.0)
        for k in range(4):
            source = (scalar_ref[i * 4 + k] // 4).astype(F32)
            extra = jnp.where(lane == 1 + k, source, extra)
        for v in range(1, 4):
            below = jnp.sum(jnp.where(notes_ref[i, 0:1, :] < v, 1.0, 0.0), axis=1, keepdims=True)
            extra = jnp.where(lane == 4 + v, below, extra)
        rows = jnp.concatenate([got_ref[scalar_ref[i * 4 + k]] for k in range(4)], axis=0)
        low_v = rows[:, 320:384]
        value = rows[:, 128:256].astype(F32) + SCALE * jnp.dot(
            low_v, wv_ref[...], preferred_element_type=F32
        )
        extra = jnp.broadcast_to(extra, (BLOCK, 64))
        out_ref[y, :, 0:128] = rows[:, 0:128]
        out_ref[y, :, 128:256] = value.astype(BF)
        out_ref[y, :, 256:384] = jnp.concatenate([low_v.astype(F32), extra], axis=1).astype(BF)


def pack(scalar, got, notes, wv):
    return pl.pallas_call(
        pack_kernel,
        out_shape=jax.ShapeDtypeStruct((4, BLOCK, 384), BF),
        in_specs=[scalars(), whole(), whole(), whole()],
        out_specs=whole(),
        cost_estimate=pl.CostEstimate(flops=1 << 23, bytes_accessed=1 << 20, transcendentals=0),
    )(scalar, got, notes, wv)


def attention_kernel(
    scalar_ref, q_ref, got_ref, d0, d1, d2, d3, notes_ref, kv_ref, wv_ref, wq_ref,
    out_ref, send_ref, send_other_ref, up_ref, up_other_ref,
    q_s, kv_s, s_s, w_s, t_s, m_s, acc_s, dq_s, dout_s, lg_s, qup_s, vup_s, send_s, up_s, below_s, sem,
):
    copies = [pltpu.make_async_copy(q_ref, q_s, sem.at[32])]
    for c in range(32):
        copies.append(
            pltpu.make_async_copy(
                kv_ref.at[c % 8, c // 8], kv_s.at[pl.ds(PAD + c * BLOCK, BLOCK), :], sem.at[c]
            )
        )
    for copy in copies:
        copy.start()
    kv_s[0:PAD, :] = jnp.zeros((PAD, 384), BF)
    t_s[...] = jnp.zeros_like(t_s)
    qup_s[...] = jnp.zeros_like(qup_s)
    vup_s[...] = jnp.zeros_like(vup_s)
    for i, d in enumerate((d0, d1, d2, d3)):
        for h in range(8):
            dout_s[i, h * BLOCK : (h + 1) * BLOCK, :] = d[:, h * HEAD : (h + 1) * HEAD]
    for copy in copies:
        copy.wait()
    counts = kv_s[PAD : PAD + 16, 256:384].astype(F32)
    for c in range(1, 32):
        counts = counts + kv_s[PAD + c * BLOCK : PAD + c * BLOCK + 16, 256:384].astype(F32)
    lane = lax.broadcasted_iota(jnp.int32, (1, 128), 1)
    below_s[0] = 0
    for v in range(1, 4):
        below_s[v] = jnp.sum(jnp.where(lane == 68 + v, counts[0:1, :], 0.0)).astype(jnp.int32)
    diagonal = lax.broadcasted_iota(jnp.int32, (BLOCK, BLOCK), 0) == lax.broadcasted_iota(
        jnp.int32, (BLOCK, BLOCK), 1
    )

    def turn_of(i, _):
        block = scalar_ref[16 + i]
        high = (block + 1) * BLOCK
        width = high - below_s[scalar_ref[20 + i]]
        steps = (width + HALF - 1) // KEY_CHUNK
        half = width > steps * KEY_CHUNK
        clean = jnp.maximum(jnp.minimum((high - below_s[scalar_ref[24 + i]]) // KEY_CHUNK, steps), 1)
        resp = notes_ref[i, 0:1, :]
        start = jnp.zeros((1, BLOCK), jnp.int32)
        for v in range(1, 4):
            start = jnp.where(resp == v, below_s[v], start)
        start = jnp.sum(jnp.where(diagonal, start.astype(F32), 0.0), axis=1, keepdims=True).astype(jnp.int32)
        start = jnp.concatenate([start] * 8, axis=0)
        row = block * BLOCK + lax.broadcasted_iota(jnp.int32, (BLOCK, 1), 0)
        row = jnp.concatenate([row] * 8, axis=0)

        chunks = [scalar_ref[i * 4 + k] for k in range(4)]
        low = jnp.concatenate([got_ref[c, :, 256:384] for c in chunks], axis=0)
        q_in = jnp.concatenate([q_s[c] for c in chunks], axis=0).astype(F32)
        query = (
            q_in + SCALE * jnp.dot(low[:, 0:64], wq_ref[...], preferred_element_type=F32)
        ).astype(BF)
        query = jnp.concatenate([query[:, h * HEAD : (h + 1) * HEAD] for h in range(8)], axis=0)
        dout = dout_s[i]

        def place(t, size):
            return pl.multiple_of(PAD + high - KEY_CHUNK * t - size, BLOCK)

        m_s[...] = jnp.full_like(m_s, MASKED)

        def scores(t, size, masked):
            at = place(t, size)
            s = lax.dot_general(query, kv_s[pl.ds(at, size), 0:128], NT, preferred_element_type=F32)
            if masked:
                key = at - PAD + lax.broadcasted_iota(jnp.int32, (1, size), 1)
                s = jnp.where((key >= start) & (key <= row), s, MASKED)
            s_s[t, :, 0:size] = s
            top = m_s[...]
            for c in range(size // 128):
                top = jnp.maximum(top, s[:, c * 128 : (c + 1) * 128])
            m_s[...] = top

        def clean_scores(t, _):
            scores(t, KEY_CHUNK, False)
            return 0

        def masked_scores(t, _):
            scores(t, KEY_CHUNK, True)
            return 0

        lax.fori_loop(0, jnp.minimum(steps, 1), masked_scores, 0)
        lax.fori_loop(1, clean, clean_scores, 0)
        lax.fori_loop(clean, steps, masked_scores, 0)

        @pl.when(half)
        def _():
            scores(steps, HALF, True)

        top = jnp.max(m_s[...], axis=1, keepdims=True)
        acc_s[...] = jnp.zeros_like(acc_s)

        def forward(t, size):
            w = jnp.exp2((s_s[t, :, 0:size] - top) * (INVERSE * LOG2E)).astype(BF)
            w_s[t, :, 0:size] = w
            acc_s[...] += jnp.dot(w, kv_s[pl.ds(place(t, size), size), 128:384], preferred_element_type=F32)

        def forward_step(t, _):
            forward(t, KEY_CHUNK)
            return 0

        lax.fori_loop(0, steps, forward_step, 0)

        @pl.when(half)
        def _():
            forward(steps, HALF)

        over = 1.0 / acc_s[:, 192:193]
        out = (acc_s[:, 0:128] * over).astype(BF)
        for h in range(8):
            out_ref[i, :, h * HEAD : (h + 1) * HEAD] = out[h * BLOCK : (h + 1) * BLOCK, :]
        wide = dout.astype(F32)
        delta = jnp.sum(wide * out.astype(F32), axis=1, keepdims=True) * over
        scaled = (wide * over).astype(BF)
        g = lax.dot_general(wv_ref[...], scaled, NT, preferred_element_type=F32).astype(BF)
        weighted_low = (acc_s[:, 128:256] * over).astype(BF)
        vup_s[...] += lax.dot_general(weighted_low, dout, TN, preferred_element_type=F32)
        dq_s[...] = jnp.zeros_like(dq_s)

        def backward(t, size):
            at = place(t, size)
            w = w_s[t, :, 0:size]
            dp = lax.dot_general(scaled, kv_s[pl.ds(at, size), 128:256], NT, preferred_element_type=F32)
            ds = (w.astype(F32) * (dp - delta)).astype(BF)
            dq_s[...] += jnp.dot(ds, kv_s[pl.ds(at, size), 0:128], preferred_element_type=F32)
            t_s[:, pl.ds(at, size)] += jnp.dot(g, w, preferred_element_type=F32)

        def backward_step(t, _):
            backward(t, KEY_CHUNK)
            return 0

        lax.fori_loop(0, steps, backward_step, 0)

        @pl.when(half)
        def _():
            backward(steps, HALF)

        dq = (dq_s[...] * INVERSE).astype(BF)
        low_t = jnp.transpose(low.astype(F32))[0:64, :].astype(BF)
        lg = jnp.zeros((64, BLOCK), F32)
        for h in range(8):
            dq_h = dq[h * BLOCK : (h + 1) * BLOCK, :]
            lg = lg + lax.dot_general(
                wq_ref[:, h * HEAD : (h + 1) * HEAD], dq_h, NT, preferred_element_type=F32
            )
            qup_s[h] += jnp.dot(low_t, dq_h, preferred_element_type=F32)
        lg_s[i] = lg
        return 0

    lax.fori_loop(0, 4, turn_of, 0)

    token_row = lax.broadcasted_iota(jnp.int32, (1, BLOCK), 1)
    token = lax.broadcasted_iota(jnp.int32, (BLOCK, BLOCK), 1)
    slot = lax.broadcasted_iota(jnp.int32, (BLOCK, BLOCK), 0)
    within = token % QUARTER == slot % QUARTER
    wanted = (slot // QUARTER).astype(F32)
    for c in range(32):
        at = (scalar_ref[28] - c // 8 + 4) % 4
        own = jnp.where(scalar_ref[16 + at] == c, 1.0, 0.0)
        both = jnp.concatenate([lg_s[at] * own, t_s[:, PAD + c * BLOCK : PAD + (c + 1) * BLOCK]], axis=0)
        both = (both * SCALE).astype(BF)
        note = kv_s[PAD + c * BLOCK : PAD + c * BLOCK + 16, 256:384].astype(F32)[0:1, :]
        source = note[:, 65:66]
        for k in range(1, 4):
            source = jnp.where(token_row // QUARTER == k, note[:, 65 + k : 66 + k], source)
        pick = jnp.where(within & (source == wanted), 1.0, 0.0).astype(BF)
        sent = lax.dot_general(pick, both, NT, preferred_element_type=F32).astype(BF)
        for g in range(4):
            send_s[c % 2, g * 16 + c // 2] = sent[g * QUARTER : (g + 1) * QUARTER, :]
    for c in range(2):
        for h in range(4):
            up_s[c, h * 64 : (h + 1) * 64, :] = (qup_s[c * 4 + h] * SCALE).astype(BF)
        up_s[c, 256:288, :] = (vup_s[c * 32 : (c + 1) * 32, :] * SCALE).astype(BF)
    core = lax.axis_index("core")
    send_ref[...] = send_s[core]
    send_other_ref[...] = send_s[1 - core]
    up_ref[...] = up_s[core]
    up_other_ref[...] = up_s[1 - core]


def attention(scalar, q, got, dout, notes, kv, wv, wq):
    chunks = 4096 // KEY_CHUNK
    return pl.pallas_call(
        attention_kernel,
        out_shape=(
            jax.ShapeDtypeStruct((4, BLOCK, 1024), BF),
            jax.ShapeDtypeStruct((64, QUARTER, 128), BF),
            jax.ShapeDtypeStruct((64, QUARTER, 128), BF),
            jax.ShapeDtypeStruct((288, 128), BF),
            jax.ShapeDtypeStruct((288, 128), BF),
        ),
        in_specs=[scalars(), pl.BlockSpec(memory_space=pl.ANY)]
        + [whole()] * 6
        + [pl.BlockSpec(memory_space=pl.ANY), whole(), whole()],
        out_specs=(whole(),) * 5,
        scratch_shapes=[
            VMEM((16, QUARTER, 1024), BF),
            VMEM((PAD + 4096, 384), BF),
            VMEM((chunks, ROWS_STEP, KEY_CHUNK), F32),
            VMEM((chunks, ROWS_STEP, KEY_CHUNK), BF),
            VMEM((64, PAD + 4096), F32),
            VMEM((ROWS_STEP, 128), F32),
            VMEM((ROWS_STEP, 256), F32),
            VMEM((ROWS_STEP, 128), F32),
            VMEM((4, ROWS_STEP, 128), BF),
            VMEM((4, 64, BLOCK), F32),
            VMEM((8, 64, 128), F32),
            VMEM((128, 128), F32),
            VMEM((2, 64, QUARTER, 128), BF),
            VMEM((2, 288, 128), BF),
            pltpu.SMEM((4,), jnp.int32),
            pltpu.SemaphoreType.DMA((33,)),
        ],
        compiler_params=params(56),
        cost_estimate=pl.CostEstimate(flops=20 << 30, bytes_accessed=8 << 20, transcendentals=8 << 20),
    )(scalar, q, got, *dout, notes, kv, wv, wq)


def low_back_kernel(route_ref, got_ref, low_ref, sum_ref):
    me = lax.axis_index("dp")
    for r in range(4):
        total = got_ref[r * 16].astype(F32)
        for c in range(1, 16):
            total = total + got_ref[r * 16 + c].astype(F32)
        sum_ref[r] = total
    outgoing = route_ref[0, pl.ds(me, 1), :]
    for k in range(4):
        low = jnp.zeros((QUARTER, 128), F32)
        for r in range(4):
            low = jnp.where(outgoing[:, k : k + 1] == r, sum_ref[r], low)
        low_ref[k * QUARTER : (k + 1) * QUARTER, :] = low.astype(BF)


def low_back_of(route, got):
    return pl.pallas_call(
        low_back_kernel,
        out_shape=jax.ShapeDtypeStruct((BLOCK, 128), BF),
        grid=(1,),
        in_specs=[
            pl.BlockSpec((1, 4, 4), lambda i: (0, 0, 0)),
            pl.BlockSpec((64, QUARTER, 128), lambda i: (0, 0, 0)),
        ],
        out_specs=pl.BlockSpec((BLOCK, 128), lambda i: (0, 0)),
        scratch_shapes=[VMEM((4, QUARTER, 128), F32)],
        cost_estimate=pl.CostEstimate(flops=1 << 19, bytes_accessed=1 << 20, transcendentals=0),
    )(route, got)


def grad_kernel(x_ref, other_ref, low_ref, low_other_ref, out_ref, own_s, sem):
    half = pl.ds(pl.multiple_of(lax.axis_index("core") * 4096, 4096), 4096)
    copy = pltpu.make_async_copy(x_ref.at[:, half], own_s, sem)
    copy.start()
    low = jnp.concatenate([low_ref[...], low_other_ref[...]], axis=0)
    copy.wait()
    for j in range(4):
        span = slice(j * 1024, (j + 1) * 1024)
        rows = jnp.concatenate([own_s[:, span], other_ref[:, span]], axis=0)
        grad = lax.dot_general(rows, low, TN, preferred_element_type=F32).astype(BF)
        for d in range(16):
            out_ref[j * 16 + d] = grad[d * 64 : (d + 1) * 64, :]


def grad_chunks(x, other, low, low_other):
    return pl.pallas_call(
        grad_kernel,
        out_shape=jax.ShapeDtypeStruct((64, 64, 128), BF),
        in_specs=[pl.BlockSpec(memory_space=pl.ANY)] + [whole()] * 3,
        out_specs=whole(),
        scratch_shapes=[VMEM((BLOCK, 4096), BF), pltpu.SemaphoreType.DMA],
        compiler_params=params(48),
        cost_estimate=pl.CostEstimate(flops=2 * 256 * 4096 * 128, bytes_accessed=4 << 20, transcendentals=0),
    )(x, other, low, low_other)


def gather_kernel(own_ref, other_ref, up_ref, up_other_ref, down_ref, query_ref, value_ref):
    zero = lax.axis_index("core") == 0
    for core in range(2):
        for chip in range(64):
            own, other = own_ref[chip].astype(F32), other_ref[chip].astype(F32)
            part = jnp.where(zero, own, other) if core == 0 else jnp.where(zero, other, own)
            down_ref[core * 4096 + chip * 64 : core * 4096 + (chip + 1) * 64, :] = part
        for y in range(4):
            own, other = up_ref[y].astype(F32), up_other_ref[y].astype(F32)
            part = jnp.where(zero, own, other) if core == 0 else jnp.where(zero, other, own)
            for h in range(4):
                column = (y * 8 + core * 4 + h) * 128
                query_ref[:, column : column + 128] = part[h * 64 : (h + 1) * 64, :]
            value_ref[core * 32 : (core + 1) * 32, y * 128 : (y + 1) * 128] = part[256:288, :]


def gather_outputs(own, other, up, up_other):
    return pl.pallas_call(
        gather_kernel,
        out_shape=(
            jax.ShapeDtypeStruct((8192, 128), F32),
            jax.ShapeDtypeStruct((64, 4096), F32),
            jax.ShapeDtypeStruct((64, 512), F32),
        ),
        in_specs=[whole()] * 4,
        out_specs=(whole(), whole(), whole()),
        compiler_params=params(32),
        cost_estimate=pl.CostEstimate(flops=1 << 20, bytes_accessed=8 << 20, transcendentals=0),
    )(own, other, up, up_other)


def join_kernel(p0, p1, p2, p3, out_ref):
    for i, piece in enumerate((p0, p1, p2, p3)):
        column = (lax.axis_index("y") + i) % 4 * 1024
        out_ref[0, :, pl.ds(pl.multiple_of(column, 1024), 1024)] = piece[...]


def join_heads(pieces):
    return pl.pallas_call(
        join_kernel,
        out_shape=jax.ShapeDtypeStruct((1, BLOCK, 4096), BF),
        grid=(1,),
        in_specs=[pl.BlockSpec((BLOCK, 1024), lambda i: (0, 0))] * 4,
        out_specs=pl.BlockSpec((1, BLOCK, 4096), lambda i: (0, 0, 0)),
        compiler_params=params(60),
        cost_estimate=pl.CostEstimate(flops=0, bytes_accessed=2 << 20, transcendentals=0),
    )(*pieces)


def on_device(
    generated_input,
    frozen_query,
    frozen_key_value,
    adapter_down_weight,
    query_up_weight,
    value_up_weight,
    response_numbers,
    target_replica,
    output_gradient,
):
    me = lax.axis_index("dp")
    my_y = lax.axis_index("y")
    my_core = lax.axis_index("core")
    my_lane = lax.axis_index("x") * 2 + my_core
    places = jnp.arange(4, dtype=jnp.int32)
    swap = [(0, 1), (1, 0)]

    rows = generated_input[0]
    sent, notes = front(target_replica, rows, adapter_down_weight, frozen_key_value[0], response_numbers)

    row = (my_y - places + 4) % 4
    notes = jnp.stack([notes] + [lax.ppermute(notes, "y", turn(d)) for d in range(1, 4)])
    resp = notes[:, 0, :]
    routes = notes[:, 1, 0:16].reshape(4, 4, 4)
    mine = (routes == me).astype(jnp.int32)
    order = (jnp.sum(mine * places[None, :, None], axis=1) * 4 + row[:, None]).reshape(16)
    block = row * 8 + my_lane
    scalar = jnp.concatenate([order, block, resp[:, 0], resp[:, 127], row]).astype(jnp.int32)

    got = lax.all_to_all(sent, ROWS, 0, 0, tiled=True)
    gradient = output_gradient[0]
    dout = []
    for d in range(4):
        part = lax.dynamic_slice_in_dim(gradient, (my_y + d) % 4 * 1024, 1024, 1)
        dout.append(lax.ppermute(part, "y", turn(d)) if d else part)
    wv = lax.dynamic_slice_in_dim(value_up_weight, my_y * 128, 128, 1)
    wq = lax.dynamic_slice_in_dim(query_up_weight, my_y * 1024, 1024, 1)
    packed = pack(scalar, got, notes, wv)
    kv = lax.all_gather(packed, ("x", "core"), axis=0, tiled=False)
    q = lax.all_to_all(
        query_chunks(target_replica, frozen_query[0]), ROWS, 0, 0, tiled=True
    )
    other_half = lax.ppermute(
        lax.dynamic_slice_in_dim(rows, (1 - my_core) * 4096, 4096, 1), "core", swap
    )

    out, send, send_other, up, up_other = attention(scalar, q, got, dout, notes, kv, wv, wq)
    pieces = [out[0]] + [lax.ppermute(out[i], "y", turn(-i)) for i in range(1, 4)]
    up_other = lax.ppermute(up_other, "core", swap)
    up = (up.astype(F32) + up_other.astype(F32)).astype(BF)
    up = sum([lax.ppermute(up, "dp", turn(d)).astype(F32) for d in range(1, 4)], up.astype(F32)).astype(BF)
    up = lax.all_gather(up, ("y", "x"), axis=0, tiled=False)
    up = jnp.sum(up.reshape(4, 4, 288, 128).astype(F32), axis=1).astype(BF)
    up_other = lax.ppermute(up, "core", swap)
    send_other = lax.ppermute(send_other, "core", swap)
    send = (send.astype(F32) + send_other.astype(F32)).astype(BF)
    low_back = low_back_of(target_replica, lax.all_to_all(send, CHIP, 0, 0, tiled=True))
    low_other = lax.ppermute(low_back, "core", swap)
    chunks = grad_chunks(rows, other_half, low_back, low_other)
    parts = lax.all_to_all(chunks, CHIP, 0, 0, tiled=True)
    shard = jnp.sum(parts.astype(F32), axis=0).astype(BF)
    shard, pieces[1], pieces[3] = lax.optimization_barrier((shard, pieces[1], pieces[3]))
    own = lax.all_to_all(jnp.broadcast_to(shard[None], parts.shape), CHIP, 0, 0, tiled=True)
    own, pieces[2], up_other = lax.optimization_barrier((own, pieces[2], up_other))
    other = lax.ppermute(own, "core", swap)
    attn_out = join_heads(pieces)
    grad_a, query_up_gradient, value_up_gradient = gather_outputs(own, other, up, up_other)

    return (attn_out, grad_a, query_up_gradient, value_up_gradient)


def solution(mesh):
    grid = Mesh(mesh.devices.reshape(4, 4, 4, 2), ("dp", "y", "x", "core"))
    ctx = ("y", "x", "core")
    return jax.shard_map(
        on_device,
        mesh=grid,
        in_specs=(
            P("dp", ctx, None),
            P("dp", ctx, None),
            P("dp", ctx, None),
            P(),
            P(),
            P(),
            P("dp", ctx),
            P(ctx, None, None),
            P("dp", ctx, None),
        ),
        out_specs=(P("dp", ctx, None), P(), P(), P()),
        check_vma=False,
    )
```

```python
import functools
import math

import jax
import jax.numpy as jnp
from jax import lax
from jax.experimental import pallas as pl
from jax.experimental.pallas import tpu as pltpu
from jax.sharding import Mesh
from jax.sharding import PartitionSpec as P

HEAD = 128
BLOCK = 128
QUARTER = 32
KEY_CHUNK = 512
HALF = KEY_CHUNK // 2
PAD = KEY_CHUNK - BLOCK
ROWS_STEP = 8 * BLOCK
SCALE = 0.5
MASKED = -1e30
INVERSE = 1.0 / math.sqrt(HEAD)
LOG2E = 1.4426950408889634
BF = jnp.bfloat16
F32 = jnp.float32
NT = (((1,), (1,)), ((), ()))
TN = (((0,), (0,)), ((), ()))
VMEM = pltpu.VMEM
CHIP = ("dp", "y", "x")
ROWS = ("dp", "y")


def turn(d):
    return [(y, (y + d) % 4) for y in range(4)]


def whole():
    return pl.BlockSpec(memory_space=pltpu.VMEM)


def scalars():
    return pl.BlockSpec(memory_space=pltpu.SMEM)


def params(mib):
    return pltpu.CompilerParams(vmem_limit_bytes=mib << 20)


def quarter_rows(route_ref, r):
    me = lax.axis_index("dp")
    quarter = sum(jnp.where(route_ref[0, me, k] == r, k, 0) for k in range(1, 4))
    return pl.ds(pl.multiple_of(quarter * QUARTER, QUARTER), QUARTER)


def front_kernel(route_ref, x_ref, a_ref, kv_ref, resp_ref, out_ref, note_ref, acc_ref, low_ref):
    step = pl.program_id(0)

    @pl.when(step == 0)
    def _():
        acc_ref[...] = jnp.zeros_like(acc_ref)

    acc_ref[...] += jnp.dot(x_ref[...], a_ref[...], preferred_element_type=F32)

    @pl.when(step == pl.num_programs(0) - 1)
    def _():
        lane = lax.broadcasted_iota(jnp.int32, (1, 128), 1)
        note = jnp.zeros((1, 128), jnp.int32)
        for g in range(4):
            for k in range(4):
                note = jnp.where(lane == g * 4 + k, route_ref[0, g, k], note)
        note_ref[0:1, :] = resp_ref[...]
        note_ref[1:2, :] = note
        low_ref[...] = acc_ref[...].astype(BF)
        for r in range(4):
            rows = quarter_rows(route_ref, r)
            low = low_ref[rows, :]
            for y in range(4):
                out_ref[r * 4 + y, :, 0:128] = kv_ref[rows, y * 128 : y * 128 + 128]
                out_ref[r * 4 + y, :, 128:256] = kv_ref[rows, 512 + y * 128 : 640 + y * 128]
                out_ref[r * 4 + y, :, 256:384] = low


def front(route, x, a, kv, resp):
    steps = 2
    part = 8192 // steps
    return pl.pallas_call(
        front_kernel,
        out_shape=(
            jax.ShapeDtypeStruct((16, QUARTER, 384), BF),
            jax.ShapeDtypeStruct((2, 128), jnp.int32),
        ),
        grid=(steps,),
        in_specs=[
            scalars(),
            pl.BlockSpec((BLOCK, part), lambda i: (0, i)),
            pl.BlockSpec((part, 128), lambda i: (i, 0)),
            pl.BlockSpec((BLOCK, 1024), lambda i: (0, 0)),
            pl.BlockSpec((1, BLOCK), lambda i: (0, 0)),
        ],
        out_specs=(
            pl.BlockSpec((16, QUARTER, 384), lambda i: (0, 0, 0)),
            pl.BlockSpec((2, 128), lambda i: (0, 0)),
        ),
        scratch_shapes=[VMEM((BLOCK, 128), F32), VMEM((BLOCK, 128), BF)],
        compiler_params=params(58),
        cost_estimate=pl.CostEstimate(flops=2 * 128 * 8192 * 128, bytes_accessed=5 << 20, transcendentals=0),
    )(route, x, a, kv, resp)


def query_chunks_kernel(route_ref, q_ref, out_ref, sem):
    copies = []
    for r in range(4):
        rows = quarter_rows(route_ref, r)
        for y in range(4):
            copies.append(
                pltpu.make_async_copy(
                    q_ref.at[rows, pl.ds(y * 1024, 1024)], out_ref.at[r * 4 + y], sem.at[r * 4 + y]
                )
            )
    for copy in copies:
        copy.start()
    for copy in copies:
        copy.wait()


def query_chunks(route, q):
    return pl.pallas_call(
        query_chunks_kernel,
        out_shape=jax.ShapeDtypeStruct((16, QUARTER, 1024), BF),
        in_specs=[scalars(), pl.BlockSpec(memory_space=pl.ANY)],
        out_specs=pl.BlockSpec(memory_space=pl.ANY),
        scratch_shapes=[pltpu.SemaphoreType.DMA((16,))],
        compiler_params=params(48),
        cost_estimate=pl.CostEstimate(flops=0, bytes_accessed=2 << 20, transcendentals=0),
    )(route, q)


def pack_kernel(scalar_ref, got_ref, notes_ref, wv_ref, out_ref):
    lane = lax.broadcasted_iota(jnp.int32, (1, 64), 1)
    for i in range(4):
        y = scalar_ref[28 + i]
        extra = jnp.where(lane == 0, 1.0, 0.0)
        for k in range(4):
            source = (scalar_ref[i * 4 + k] // 4).astype(F32)
            extra = jnp.where(lane == 1 + k, source, extra)
        for v in range(1, 4):
            below = jnp.sum(jnp.where(notes_ref[i, 0:1, :] < v, 1.0, 0.0), axis=1, keepdims=True)
            extra = jnp.where(lane == 4 + v, below, extra)
        rows = jnp.concatenate([got_ref[scalar_ref[i * 4 + k]] for k in range(4)], axis=0)
        low_v = rows[:, 320:384]
        value = rows[:, 128:256].astype(F32) + SCALE * jnp.dot(
            low_v, wv_ref[...], preferred_element_type=F32
        )
        extra = jnp.broadcast_to(extra, (BLOCK, 64))
        out_ref[y, :, 0:128] = rows[:, 0:128]
        out_ref[y, :, 128:256] = value.astype(BF)
        out_ref[y, :, 256:384] = jnp.concatenate([low_v.astype(F32), extra], axis=1).astype(BF)


def pack(scalar, got, notes, wv):
    return pl.pallas_call(
        pack_kernel,
        out_shape=jax.ShapeDtypeStruct((4, BLOCK, 384), BF),
        in_specs=[scalars(), whole(), whole(), whole()],
        out_specs=whole(),
        cost_estimate=pl.CostEstimate(flops=1 << 23, bytes_accessed=1 << 20, transcendentals=0),
    )(scalar, got, notes, wv)


def attention_kernel(
    scalar_ref, q_ref, got_ref, d0, d1, d2, d3, notes_ref, kv_ref, wv_ref, wq_ref,
    out_ref, send_ref, send_other_ref, up_ref, up_other_ref,
    q_s, kv_s, s_s, w_s, t_s, m_s, acc_s, dq_s, dout_s, lg_s, qup_s, vup_s, send_s, up_s, below_s, sem,
):
    copies = [pltpu.make_async_copy(q_ref, q_s, sem.at[32])]
    for c in range(32):
        copies.append(
            pltpu.make_async_copy(
                kv_ref.at[c % 8, c // 8], kv_s.at[pl.ds(PAD + c * BLOCK, BLOCK), :], sem.at[c]
            )
        )
    for copy in copies:
        copy.start()
    kv_s[0:PAD, :] = jnp.zeros((PAD, 384), BF)
    t_s[...] = jnp.zeros_like(t_s)
    qup_s[...] = jnp.zeros_like(qup_s)
    vup_s[...] = jnp.zeros_like(vup_s)
    for i, d in enumerate((d0, d1, d2, d3)):
        for h in range(8):
            dout_s[i, h * BLOCK : (h + 1) * BLOCK, :] = d[:, h * HEAD : (h + 1) * HEAD]
    for copy in copies:
        copy.wait()
    counts = kv_s[PAD : PAD + 16, 256:384].astype(F32)
    for c in range(1, 32):
        counts = counts + kv_s[PAD + c * BLOCK : PAD + c * BLOCK + 16, 256:384].astype(F32)
    lane = lax.broadcasted_iota(jnp.int32, (1, 128), 1)
    below_s[0] = 0
    for v in range(1, 4):
        below_s[v] = jnp.sum(jnp.where(lane == 68 + v, counts[0:1, :], 0.0)).astype(jnp.int32)
    diagonal = lax.broadcasted_iota(jnp.int32, (BLOCK, BLOCK), 0) == lax.broadcasted_iota(
        jnp.int32, (BLOCK, BLOCK), 1
    )

    def turn_of(i, _):
        block = scalar_ref[16 + i]
        high = (block + 1) * BLOCK
        width = high - below_s[scalar_ref[20 + i]]
        steps = (width + HALF - 1) // KEY_CHUNK
        half = width > steps * KEY_CHUNK
        clean = jnp.maximum(jnp.minimum((high - below_s[scalar_ref[24 + i]]) // KEY_CHUNK, steps), 1)
        resp = notes_ref[i, 0:1, :]
        start = jnp.zeros((1, BLOCK), jnp.int32)
        for v in range(1, 4):
            start = jnp.where(resp == v, below_s[v], start)
        start = jnp.sum(jnp.where(diagonal, start.astype(F32), 0.0), axis=1, keepdims=True).astype(jnp.int32)
        start = jnp.concatenate([start] * 8, axis=0)
        row = block * BLOCK + lax.broadcasted_iota(jnp.int32, (BLOCK, 1), 0)
        row = jnp.concatenate([row] * 8, axis=0)

        chunks = [scalar_ref[i * 4 + k] for k in range(4)]
        low = jnp.concatenate([got_ref[c, :, 256:384] for c in chunks], axis=0)
        q_in = jnp.concatenate([q_s[c] for c in chunks], axis=0).astype(F32)
        query = (
            q_in + SCALE * jnp.dot(low[:, 0:64], wq_ref[...], preferred_element_type=F32)
        ).astype(BF)
        query = jnp.concatenate([query[:, h * HEAD : (h + 1) * HEAD] for h in range(8)], axis=0)
        dout = dout_s[i]

        def place(t, size):
            return pl.multiple_of(PAD + high - KEY_CHUNK * t - size, BLOCK)

        m_s[...] = jnp.full_like(m_s, MASKED)

        def scores(t, size, masked):
            at = place(t, size)
            s = lax.dot_general(query, kv_s[pl.ds(at, size), 0:128], NT, preferred_element_type=F32)
            if masked:
                key = at - PAD + lax.broadcasted_iota(jnp.int32, (1, size), 1)
                s = jnp.where((key >= start) & (key <= row), s, MASKED)
            s_s[t, :, 0:size] = s
            top = m_s[...]
            for c in range(size // 128):
                top = jnp.maximum(top, s[:, c * 128 : (c + 1) * 128])
            m_s[...] = top

        def clean_scores(t, _):
            scores(t, KEY_CHUNK, False)
            return 0

        def masked_scores(t, _):
            scores(t, KEY_CHUNK, True)
            return 0

        lax.fori_loop(0, jnp.minimum(steps, 1), masked_scores, 0)
        lax.fori_loop(1, clean, clean_scores, 0)
        lax.fori_loop(clean, steps, masked_scores, 0)

        @pl.when(half)
        def _():
            scores(steps, HALF, True)

        top = jnp.max(m_s[...], axis=1, keepdims=True)
        acc_s[...] = jnp.zeros_like(acc_s)

        def forward(t, size):
            w = jnp.exp2((s_s[t, :, 0:size] - top) * (INVERSE * LOG2E)).astype(BF)
            w_s[t, :, 0:size] = w
            acc_s[...] += jnp.dot(w, kv_s[pl.ds(place(t, size), size), 128:384], preferred_element_type=F32)

        def forward_step(t, _):
            forward(t, KEY_CHUNK)
            return 0

        lax.fori_loop(0, steps, forward_step, 0)

        @pl.when(half)
        def _():
            forward(steps, HALF)

        over = 1.0 / acc_s[:, 192:193]
        out = (acc_s[:, 0:128] * over).astype(BF)
        for h in range(8):
            out_ref[i, :, h * HEAD : (h + 1) * HEAD] = out[h * BLOCK : (h + 1) * BLOCK, :]
        wide = dout.astype(F32)
        delta = jnp.sum(wide * out.astype(F32), axis=1, keepdims=True) * over
        scaled = (wide * over).astype(BF)
        g = lax.dot_general(wv_ref[...], scaled, NT, preferred_element_type=F32).astype(BF)
        weighted_low = (acc_s[:, 128:256] * over).astype(BF)
        vup_s[...] += lax.dot_general(weighted_low, dout, TN, preferred_element_type=F32)
        dq_s[...] = jnp.zeros_like(dq_s)

        def backward(t, size):
            at = place(t, size)
            w = w_s[t, :, 0:size]
            dp = lax.dot_general(scaled, kv_s[pl.ds(at, size), 128:256], NT, preferred_element_type=F32)
            ds = (w.astype(F32) * (dp - delta)).astype(BF)
            dq_s[...] += jnp.dot(ds, kv_s[pl.ds(at, size), 0:128], preferred_element_type=F32)
            t_s[:, pl.ds(at, size)] += jnp.dot(g, w, preferred_element_type=F32)

        def backward_step(t, _):
            backward(t, KEY_CHUNK)
            return 0

        lax.fori_loop(0, steps, backward_step, 0)

        @pl.when(half)
        def _():
            backward(steps, HALF)

        dq = (dq_s[...] * INVERSE).astype(BF)
        low_t = jnp.transpose(low.astype(F32))[0:64, :].astype(BF)
        lg = jnp.zeros((64, BLOCK), F32)
        for h in range(8):
            dq_h = dq[h * BLOCK : (h + 1) * BLOCK, :]
            lg = lg + lax.dot_general(
                wq_ref[:, h * HEAD : (h + 1) * HEAD], dq_h, NT, preferred_element_type=F32
            )
            qup_s[h] += jnp.dot(low_t, dq_h, preferred_element_type=F32)
        lg_s[i] = lg
        return 0

    lax.fori_loop(0, 4, turn_of, 0)

    token_row = lax.broadcasted_iota(jnp.int32, (1, BLOCK), 1)
    token = lax.broadcasted_iota(jnp.int32, (BLOCK, BLOCK), 1)
    slot = lax.broadcasted_iota(jnp.int32, (BLOCK, BLOCK), 0)
    within = token % QUARTER == slot % QUARTER
    wanted = (slot // QUARTER).astype(F32)
    for c in range(32):
        at = (scalar_ref[28] - c // 8 + 4) % 4
        own = jnp.where(scalar_ref[16 + at] == c, 1.0, 0.0)
        both = jnp.concatenate([lg_s[at] * own, t_s[:, PAD + c * BLOCK : PAD + (c + 1) * BLOCK]], axis=0)
        both = (both * SCALE).astype(BF)
        note = kv_s[PAD + c * BLOCK : PAD + c * BLOCK + 16, 256:384].astype(F32)[0:1, :]
        source = note[:, 65:66]
        for k in range(1, 4):
            source = jnp.where(token_row // QUARTER == k, note[:, 65 + k : 66 + k], source)
        pick = jnp.where(within & (source == wanted), 1.0, 0.0).astype(BF)
        sent = lax.dot_general(pick, both, NT, preferred_element_type=F32).astype(BF)
        for g in range(4):
            send_s[c % 2, g * 16 + c // 2] = sent[g * QUARTER : (g + 1) * QUARTER, :]
    for c in range(2):
        for h in range(4):
            up_s[c, h * 64 : (h + 1) * 64, :] = (qup_s[c * 4 + h] * SCALE).astype(BF)
        up_s[c, 256:288, :] = (vup_s[c * 32 : (c + 1) * 32, :] * SCALE).astype(BF)
    core = lax.axis_index("core")
    send_ref[...] = send_s[core]
    send_other_ref[...] = send_s[1 - core]
    up_ref[...] = up_s[core]
    up_other_ref[...] = up_s[1 - core]


def attention(scalar, q, got, dout, notes, kv, wv, wq):
    chunks = 4096 // KEY_CHUNK
    return pl.pallas_call(
        attention_kernel,
        out_shape=(
            jax.ShapeDtypeStruct((4, BLOCK, 1024), BF),
            jax.ShapeDtypeStruct((64, QUARTER, 128), BF),
            jax.ShapeDtypeStruct((64, QUARTER, 128), BF),
            jax.ShapeDtypeStruct((288, 128), BF),
            jax.ShapeDtypeStruct((288, 128), BF),
        ),
        in_specs=[scalars(), pl.BlockSpec(memory_space=pl.ANY)]
        + [whole()] * 6
        + [pl.BlockSpec(memory_space=pl.ANY), whole(), whole()],
        out_specs=(whole(),) * 5,
        scratch_shapes=[
            VMEM((16, QUARTER, 1024), BF),
            VMEM((PAD + 4096, 384), BF),
            VMEM((chunks, ROWS_STEP, KEY_CHUNK), F32),
            VMEM((chunks, ROWS_STEP, KEY_CHUNK), BF),
            VMEM((64, PAD + 4096), F32),
            VMEM((ROWS_STEP, 128), F32),
            VMEM((ROWS_STEP, 256), F32),
            VMEM((ROWS_STEP, 128), F32),
            VMEM((4, ROWS_STEP, 128), BF),
            VMEM((4, 64, BLOCK), F32),
            VMEM((8, 64, 128), F32),
            VMEM((128, 128), F32),
            VMEM((2, 64, QUARTER, 128), BF),
            VMEM((2, 288, 128), BF),
            pltpu.SMEM((4,), jnp.int32),
            pltpu.SemaphoreType.DMA((33,)),
        ],
        compiler_params=params(56),
        cost_estimate=pl.CostEstimate(flops=20 << 30, bytes_accessed=8 << 20, transcendentals=8 << 20),
    )(scalar, q, got, *dout, notes, kv, wv, wq)


def low_back_kernel(route_ref, got_ref, low_ref, sum_ref):
    me = lax.axis_index("dp")
    for r in range(4):
        total = got_ref[r * 16].astype(F32)
        for c in range(1, 16):
            total = total + got_ref[r * 16 + c].astype(F32)
        sum_ref[r] = total
    outgoing = route_ref[0, pl.ds(me, 1), :]
    for k in range(4):
        low = jnp.zeros((QUARTER, 128), F32)
        for r in range(4):
            low = jnp.where(outgoing[:, k : k + 1] == r, sum_ref[r], low)
        low_ref[k * QUARTER : (k + 1) * QUARTER, :] = low.astype(BF)


def low_back_of(route, got):
    return pl.pallas_call(
        low_back_kernel,
        out_shape=jax.ShapeDtypeStruct((BLOCK, 128), BF),
        grid=(1,),
        in_specs=[
            pl.BlockSpec((1, 4, 4), lambda i: (0, 0, 0)),
            pl.BlockSpec((64, QUARTER, 128), lambda i: (0, 0, 0)),
        ],
        out_specs=pl.BlockSpec((BLOCK, 128), lambda i: (0, 0)),
        scratch_shapes=[VMEM((4, QUARTER, 128), F32)],
        cost_estimate=pl.CostEstimate(flops=1 << 19, bytes_accessed=1 << 20, transcendentals=0),
    )(route, got)


def grad_kernel(x_ref, other_ref, low_ref, low_other_ref, out_ref, own_s, sem):
    half = pl.ds(pl.multiple_of(lax.axis_index("core") * 4096, 4096), 4096)
    copy = pltpu.make_async_copy(x_ref.at[:, half], own_s, sem)
    copy.start()
    low = jnp.concatenate([low_ref[...], low_other_ref[...]], axis=0)
    copy.wait()
    for j in range(4):
        span = slice(j * 1024, (j + 1) * 1024)
        rows = jnp.concatenate([own_s[:, span], other_ref[:, span]], axis=0)
        grad = lax.dot_general(rows, low, TN, preferred_element_type=F32).astype(BF)
        for d in range(16):
            out_ref[j * 16 + d] = grad[d * 64 : (d + 1) * 64, :]


def grad_chunks(x, other, low, low_other):
    return pl.pallas_call(
        grad_kernel,
        out_shape=jax.ShapeDtypeStruct((64, 64, 128), BF),
        in_specs=[pl.BlockSpec(memory_space=pl.ANY)] + [whole()] * 3,
        out_specs=whole(),
        scratch_shapes=[VMEM((BLOCK, 4096), BF), pltpu.SemaphoreType.DMA],
        compiler_params=params(48),
        cost_estimate=pl.CostEstimate(flops=2 * 256 * 4096 * 128, bytes_accessed=4 << 20, transcendentals=0),
    )(x, other, low, low_other)


def gather_kernel(own_ref, other_ref, up_ref, up_other_ref, down_ref, query_ref, value_ref):
    zero = lax.axis_index("core") == 0
    for core in range(2):
        for chip in range(64):
            own, other = own_ref[chip].astype(F32), other_ref[chip].astype(F32)
            part = jnp.where(zero, own, other) if core == 0 else jnp.where(zero, other, own)
            down_ref[core * 4096 + chip * 64 : core * 4096 + (chip + 1) * 64, :] = part
        for y in range(4):
            own, other = up_ref[y].astype(F32), up_other_ref[y].astype(F32)
            part = jnp.where(zero, own, other) if core == 0 else jnp.where(zero, other, own)
            for h in range(4):
                column = (y * 8 + core * 4 + h) * 128
                query_ref[:, column : column + 128] = part[h * 64 : (h + 1) * 64, :]
            value_ref[core * 32 : (core + 1) * 32, y * 128 : (y + 1) * 128] = part[256:288, :]


def gather_outputs(own, other, up, up_other):
    return pl.pallas_call(
        gather_kernel,
        out_shape=(
            jax.ShapeDtypeStruct((8192, 128), F32),
            jax.ShapeDtypeStruct((64, 4096), F32),
            jax.ShapeDtypeStruct((64, 512), F32),
        ),
        in_specs=[whole()] * 4,
        out_specs=(whole(), whole(), whole()),
        compiler_params=params(32),
        cost_estimate=pl.CostEstimate(flops=1 << 20, bytes_accessed=8 << 20, transcendentals=0),
    )(own, other, up, up_other)


def join_kernel(p0, p1, p2, p3, out_ref):
    for i, piece in enumerate((p0, p1, p2, p3)):
        column = (lax.axis_index("y") + i) % 4 * 1024
        out_ref[0, :, pl.ds(pl.multiple_of(column, 1024), 1024)] = piece[...]


def join_heads(pieces):
    return pl.pallas_call(
        join_kernel,
        out_shape=jax.ShapeDtypeStruct((1, BLOCK, 4096), BF),
        grid=(1,),
        in_specs=[pl.BlockSpec((BLOCK, 1024), lambda i: (0, 0))] * 4,
        out_specs=pl.BlockSpec((1, BLOCK, 4096), lambda i: (0, 0, 0)),
        compiler_params=params(60),
        cost_estimate=pl.CostEstimate(flops=0, bytes_accessed=2 << 20, transcendentals=0),
    )(*pieces)


def on_device(
    generated_input,
    frozen_query,
    frozen_key_value,
    adapter_down_weight,
    query_up_weight,
    value_up_weight,
    response_numbers,
    target_replica,
    output_gradient,
):
    me = lax.axis_index("dp")
    my_y = lax.axis_index("y")
    my_core = lax.axis_index("core")
    my_lane = lax.axis_index("x") * 2 + my_core
    places = jnp.arange(4, dtype=jnp.int32)
    swap = [(0, 1), (1, 0)]

    rows = generated_input[0]
    sent, notes = front(target_replica, rows, adapter_down_weight, frozen_key_value[0], response_numbers)

    row = (my_y - places + 4) % 4
    notes = jnp.stack([notes] + [lax.ppermute(notes, "y", turn(d)) for d in range(1, 4)])
    resp = notes[:, 0, :]
    routes = notes[:, 1, 0:16].reshape(4, 4, 4)
    mine = (routes == me).astype(jnp.int32)
    order = (jnp.sum(mine * places[None, :, None], axis=1) * 4 + row[:, None]).reshape(16)
    block = row * 8 + my_lane
    scalar = jnp.concatenate([order, block, resp[:, 0], resp[:, 127], row]).astype(jnp.int32)

    got = lax.all_to_all(sent, ROWS, 0, 0, tiled=True)
    gradient = output_gradient[0]
    dout = []
    for d in range(4):
        part = lax.dynamic_slice_in_dim(gradient, (my_y + d) % 4 * 1024, 1024, 1)
        dout.append(lax.ppermute(part, "y", turn(d)) if d else part)
    wv = lax.dynamic_slice_in_dim(value_up_weight, my_y * 128, 128, 1)
    wq = lax.dynamic_slice_in_dim(query_up_weight, my_y * 1024, 1024, 1)
    packed = pack(scalar, got, notes, wv)
    kv = lax.all_gather(packed, ("x", "core"), axis=0, tiled=False)
    q = lax.all_to_all(
        query_chunks(target_replica, frozen_query[0]), ROWS, 0, 0, tiled=True
    )
    other_half = lax.ppermute(
        lax.dynamic_slice_in_dim(rows, (1 - my_core) * 4096, 4096, 1), "core", swap
    )

    out, send, send_other, up, up_other = attention(scalar, q, got, dout, notes, kv, wv, wq)
    pieces = [out[0]] + [lax.ppermute(out[i], "y", turn(-i)) for i in range(1, 4)]
    up_other = lax.ppermute(up_other, "core", swap)
    up = (up.astype(F32) + up_other.astype(F32)).astype(BF)
    up = sum([lax.ppermute(up, "dp", turn(d)).astype(F32) for d in range(1, 4)], up.astype(F32)).astype(BF)
    up = lax.all_gather(up, ("y", "x"), axis=0, tiled=False)
    up = jnp.sum(up.reshape(4, 4, 288, 128).astype(F32), axis=1).astype(BF)
    up_other = lax.ppermute(up, "core", swap)
    send_other = lax.ppermute(send_other, "core", swap)
    send = (send.astype(F32) + send_other.astype(F32)).astype(BF)
    low_back = low_back_of(target_replica, lax.all_to_all(send, CHIP, 0, 0, tiled=True))
    low_other = lax.ppermute(low_back, "core", swap)
    chunks = grad_chunks(rows, other_half, low_back, low_other)
    chunks, pieces[1], pieces[3] = lax.optimization_barrier((chunks, pieces[1], pieces[3]))
    parts = lax.all_to_all(chunks, CHIP, 0, 0, tiled=True)
    shard = jnp.sum(parts.astype(F32), axis=0).astype(BF)
    own = lax.all_to_all(jnp.broadcast_to(shard[None], parts.shape), CHIP, 0, 0, tiled=True)
    own, pieces[2], up_other = lax.optimization_barrier((own, pieces[2], up_other))
    other = lax.ppermute(own, "core", swap)
    attn_out = join_heads(pieces)
    grad_a, query_up_gradient, value_up_gradient = gather_outputs(own, other, up, up_other)

    return (attn_out, grad_a, query_up_gradient, value_up_gradient)


def solution(mesh):
    grid = Mesh(mesh.devices.reshape(4, 4, 4, 2), ("dp", "y", "x", "core"))
    ctx = ("y", "x", "core")
    return jax.shard_map(
        on_device,
        mesh=grid,
        in_specs=(
            P("dp", ctx, None),
            P("dp", ctx, None),
            P("dp", ctx, None),
            P(),
            P(),
            P(),
            P("dp", ctx),
            P(ctx, None, None),
            P("dp", ctx, None),
        ),
        out_specs=(P("dp", ctx, None), P(), P(), P()),
        check_vma=False,
    )
```
